256 devices in a mesh: layer: 8 (over z), latent: 16 (over x, y_hi, core), tok: 2 (over y_lo).
Axes of the slice: x: 4, y: 4 (y_hi: 2, y_lo: 2; y = y_hi * 2 + y_lo), z: 8, core: 2. Of those that a mesh axis runs over, the one named last changes fastest.
Arguments:
- layer_inputs: bfloat16 [8, 512, 2048], P('layer', 'tok'), may hold values from -6 to 6
- layer_targets: bfloat16 [8, 512, 2048], P('layer', ('latent', 'tok')), may hold values from -6 to 6
- encoder_weight: bfloat16 [8, 2048, 4096], P('layer', None, 'latent'), may hold values from -0.125 to 0.125
- encoder_bias: float32 [8, 4096], P('layer', 'latent'), may hold values from -1 to 1
- decoder_weight: bfloat16 [8, 4, 2, 4096, 2048], P('layer', None, 'tok', 'latent'), may hold values from -0.03125 to 0.03125
Outputs:
- reconstruction: bfloat16 [8, 512, 2048], P('layer', ('latent', 'tok'))
- encoder_grad: bfloat16 [8, 2048, 4096], P('layer', None, 'latent')
- bias_grad: float32 [8, 4096], P('layer', 'latent')
- decoder_grad: bfloat16 [8, 4, 2, 4096, 2048], P('layer', None, 'tok', 'latent')
The draws below stay inside these ranges and needn't reach their ends.
All inputs are finite; a program needn't handle non-finite values.
Results may differ from the reference program's by a relative error of at most 0.0053.
Values may be sent and summed in bfloat16 or wider, within the bound.
A program may use at most 128 MiB of HBM per device.

```python
import jax
import jax.numpy as jnp
from jax import lax

D = 2048
F = 4096
LAYERS = 8
TOKENS = 512
SRC_SETS = 2
SRC_PER = 4


def level_of(rng, extent, cuts, low, high):
    gain = 1.0
    for position, blocks in cuts:
        steps = jax.random.uniform(jax.random.fold_in(jax.random.fold_in(rng, 6), position), (blocks,), jnp.float32, low / len(cuts), high / len(cuts))
        gain = gain * jnp.repeat(jnp.exp(steps), extent[position] // blocks).reshape((-1,) + (1,) * (len(extent) - 1 - position))
    return gain


def bell_draw(stream_key, extent, scale, most, pieces=(), held_as=jnp.bfloat16):
    entries = jax.random.normal(stream_key, extent, jnp.float32) * scale
    if len(pieces) > 0:
        entries = level_of(stream_key, extent, pieces, -0.22, 0.18) * entries
    return jnp.clip(entries, min=-most, max=most).astype(held_as)


def setup_inputs(seed: int = 0) -> dict:
    splits = jax.random.split(jax.random.key(seed), 6)
    layer_inputs = bell_draw(splits[0], (LAYERS, TOKENS, D), 1.0, 6.0, ((0, 8), (1, 2)))
    layer_targets = bell_draw(splits[1], (LAYERS, TOKENS, D), 1.0, 6.0, ((0, 8), (1, 32)))
    encoder_weight = bell_draw(splits[2], (LAYERS, D, F), D ** -0.5, 0.125, ((0, 8), (2, 16)))
    encoder_bias = jnp.clip(jax.random.uniform(splits[3], (LAYERS, F), jnp.float32, -1.0, 1.0) * level_of(splits[3], (LAYERS, F), ((0, 8), (1, 16)), -0.4, 0.0), -1.0, 1.0)
    decoder_weight = bell_draw(splits[4], (LAYERS, SRC_PER, SRC_SETS, F, D), (F * LAYERS) ** -0.5, 0.03125, ((0, 8), (2, 2), (3, 16)))
    return {"layer_inputs": layer_inputs, "layer_targets": layer_targets, "encoder_weight": encoder_weight, "encoder_bias": encoder_bias, "decoder_weight": decoder_weight}


def smooth_gate(values):
    return jax.nn.gelu(values, approximate=True)

def reference(layer_inputs, layer_targets, encoder_weight, encoder_bias, decoder_weight):
    preacts = []
    latents = []
    for source in range(LAYERS):
        preact = jnp.dot(layer_inputs[source], encoder_weight[source], preferred_element_type=jnp.float32) + encoder_bias[source]
        preacts.append(preact)
        latents.append(smooth_gate(preact).astype(jnp.bfloat16))

    def block(target, source):
        return decoder_weight[target, source // SRC_SETS, source % SRC_SETS]
    recon_list = []
    errors = []
    for target in range(LAYERS):
        total = jnp.zeros((TOKENS, D), jnp.float32)
        for source in range(target + 1):
            total = total + jnp.dot(latents[source], block(target, source), preferred_element_type=jnp.float32)
        recon_list.append(total.astype(jnp.bfloat16))
        errors.append(total - layer_targets[target].astype(jnp.float32))
    reconstruction = jnp.stack(recon_list)
    decoder_rows = []
    for target in range(LAYERS):
        blocks = []
        for source in range(LAYERS):
            if source <= target:
                blocks.append(jnp.dot(latents[source].astype(jnp.float32).T, errors[target], precision=lax.Precision.HIGHEST, preferred_element_type=jnp.float32).astype(jnp.bfloat16))
            else:
                blocks.append(jnp.zeros((F, D), jnp.bfloat16))
        decoder_rows.append(jnp.stack(blocks).reshape(SRC_PER, SRC_SETS, F, D))
    decoder_grad = jnp.stack(decoder_rows)
    encoder_rows = []
    bias_rows = []
    for source in range(LAYERS):
        latent_grad = jnp.zeros((TOKENS, F), jnp.float32)
        for target in range(source, LAYERS):
            latent_grad = latent_grad + jnp.dot(errors[target], block(target, source).astype(jnp.float32).T, precision=lax.Precision.HIGHEST, preferred_element_type=jnp.float32)
        unused, pullback = jax.vjp(smooth_gate, preacts[source])
        preact_grad = pullback(latent_grad)[0]
        encoder_rows.append(jnp.dot(layer_inputs[source].T, preact_grad.astype(jnp.bfloat16), preferred_element_type=jnp.float32).astype(jnp.bfloat16))
        bias_rows.append(lax.optimization_barrier(jnp.sum(preact_grad, axis=0)))
    return (reconstruction, jnp.stack(encoder_rows), jnp.stack(bias_rows), decoder_grad)
```

```python
import jax
import jax.numpy as jnp
from jax import lax
from jax.experimental import pallas as pl
from jax.experimental.pallas import tpu as pltpu
from jax.sharding import PartitionSpec as P

MESH = pl.DeviceIdType.MESH
BF = jnp.bfloat16
F32 = jnp.float32


def mul(value, by):
    return pl.multiple_of(value * by, by)


class Numbers:
    def __init__(self):
        self.count = 0

    def take(self, n=1):
        base = self.count
        self.count += n
        return base


def kernel(
    x_hbm, t_ref, we_hbm, b_ref, w_hbm,
    rec_ref, enc_hbm, bias_ref, dec_hbm,
    xp, xt, we, wp, own, latb, lt, gp, tg, p32, cs, cr, s32, ys, ra, rb, u32, xs, rx, rc, err,
    term, gr, gs, lg, pg, bs, recs, encv, dg, ss, rs, ls,
):
    z, lat, k = lax.axis_index("layer"), lax.axis_index("latent"), lax.axis_index("tok")
    x, yh, c = lat // 4, (lat // 2) % 2, lat % 2
    y = yh * 2 + k
    h = z % 2
    o = 1 - c

    def dev(dx=0, dy=0, dz=0, flip=0):
        xx, yy, zz = (x + dx) % 4, (y + dy) % 4, (z + dz) % 8
        cc = o if flip else c
        return (zz, xx * 4 + (yy // 2) * 2 + cc, yy % 2)

    mate = (z, lat, 1 - k)
    snum, rnum, lnum = Numbers(), Numbers(), Numbers()
    late = []

    def rc_(src, dst, si, ri, to):
        return pltpu.make_async_remote_copy(
            src_ref=src, dst_ref=dst, send_sem=ss.at[si], recv_sem=rs.at[ri],
            device_id=to, device_id_type=MESH,
        )

    def send(src, dst, ri, to, cond=None, si=None):
        si = snum.take() if si is None else si
        copy = rc_(src, dst, si, ri, to)
        if cond is None:
            copy.start()
        else:
            pl.when(cond)(copy.start)
        late.append((copy, cond))

    def arrived(dst, ri, cond=None):
        copy = rc_(dst, dst, 0, ri, mate)
        if cond is None:
            copy.wait_recv()
        else:
            pl.when(cond)(copy.wait_recv)

    def local(src, dst):
        copy = pltpu.make_async_copy(src, dst, ls.at[lnum.take()])
        copy.start()
        return copy

    load_x = [[local(x_hbm.at[:, :, cc, q], xp.at[q, k, cc]) for cc in range(2)] for q in range(2)]
    load_we = local(we_hbm, we)
    load_w = [
        local(
            w_hbm.at[:, hh * 1024 + ab * 512 : hh * 1024 + ab * 512 + 512],
            wp.at[:, ab * 1024 + hh * 512 : ab * 1024 + hh * 512 + 512],
        )
        for ab in range(2)
        for hh in range(2)
    ]

    barrier = pltpu.get_barrier_semaphore()
    peers = [dev(dz=1), dev(dz=-1), dev(flip=1)]
    peers += [dev(dy=d) for d in (1, 2, 3)] + [dev(dx=d) for d in (1, 2, 3)]
    for to in peers:
        pl.semaphore_signal(barrier, inc=1, device_id=to, device_id_type=MESH)

    ku = [4, 4, 3 - k, 1 - k]
    kd = [3, 3 * (1 - k), 0, 0]
    route = []
    for m in range(4):
        s = 2 * m + k
        u, d = z - s, (s - z + 8) % 8
        on_up = jnp.logical_and(u >= 1, u <= ku[m])
        on_dn = jnp.logical_and(d >= 1, d <= kd[m])
        on = jnp.logical_or(on_up, on_dn)
        dist = jnp.where(on_up, u, d)
        reach = jnp.where(on_up, ku[m], kd[m])
        passing = jnp.logical_and(on_dn, z < s)
        next_passing = jnp.logical_and(on_dn, (z + 7) % 8 < s)
        next_passing = jnp.logical_and(next_passing, z > 0)
        route.append(dict(on=on, up=on_up, dn=on_dn, dist=dist, reach=reach, passing=passing,
                          next_passing=next_passing, valid=s <= z,
                          onward=jnp.where(on_up, 1, 7), back=jnp.where(on_up, 7, 1)))
    mine = z // 2
    home = k == h
    ku_own = jnp.where(mine == 0, 4, jnp.where(mine == 1, 4, jnp.where(mine == 2, 3 - k, 1 - k)))
    kd_own = jnp.where(mine == 0, 3, jnp.where(mine == 1, 3 * (1 - k), 0))
    home_up = jnp.logical_and(home, ku_own > 0)
    home_dn = jnp.logical_and(home, kd_own > 0)
    away = jnp.logical_not(home)

    for m in range(4):
        @pl.when(jnp.logical_not(route[m]["valid"]))
        def _():
            latb[m] = jnp.zeros((512, 256), BF)

    lat_r = rnum.take(16)
    mate_x, core_x, mate_t, mate_rec, mate_bias = (rnum.take() for _ in range(5))
    pg_r = rnum.take(4)
    gr_r = rnum.take(20)

    def lat_sem(m, q, j):
        return lat_r + m * 4 + q * 2 + j

    def rows(q, j):
        kk = k if j == 0 else 1 - k
        return pl.ds(pl.multiple_of(q * 256 + kk * 128, 128), 128)

    def origin_send(q, j):
        r = rows(q, j)
        src = latb.at[mine, r]
        send(src, src, lat_sem(mine, q, j), dev(dz=1), home_up)
        slot = jnp.where(jnp.logical_and(z >= 1, z - 1 < z), 4, mine)
        send(src, latb.at[slot, r], lat_sem(mine, q, j), dev(dz=-1), home_dn)

    def gate(v):
        inner = 0.7978845608028654 * (v + 0.044715 * (v * v * v))
        t = jnp.tanh(inner)
        cdf = 0.5 * (1.0 + t)
        slope = cdf + 0.5 * v * (1.0 - t * t) * (0.7978845608028654 * (1.0 + 0.134145 * (v * v)))
        return v * cdf, slope

    def preact(q, kk):
        v = jnp.dot(xp[q, kk].reshape(128, 2048), we[...], preferred_element_type=F32) + b_ref[...]
        return gate(v)

    load_we.wait()
    for q in range(2):
        for copy in load_x[q]:
            copy.wait()
        val, slope = preact(q, k)
        val = val.astype(BF)
        own[q] = val
        gp[rows(q, 0), :] = slope

        @pl.when(home)
        def _():
            latb[mine, rows(q, 0), :] = val

        if q == 0:
            pl.semaphore_wait(barrier, len(peers))
        send(own.at[q], latb.at[mine, rows(q, 0)], lat_sem(mine, q, 1), mate, away)
        origin_send(q, 0)

    tg[k] = t_ref[:, pl.ds(mul(k, 1024), 1024)]
    send(t_ref.at[:, pl.ds(mul(1 - k, 1024), 1024)], tg.at[k], mate_t, mate)
    send(xp.at[c, k], xp.at[c, k], mate_x, mate)

    def lat_relay(q):
        for j in range(2):
            if j == 1:
                arrived(latb.at[mine, rows(q, 1)], lat_sem(mine, q, 1), home)
                origin_send(q, 1)
        for far in (1, 2, 3):
            for j in range(2):
                for m in range(3):
                    if far == 3 and m == 2:
                        continue
                    e = route[m]
                    cond = jnp.logical_and(e["on"], jnp.logical_and(e["dist"] == far, e["dist"] < e["reach"]))
                    src = latb.at[jnp.where(e["passing"], 4, m), rows(q, j)]
                    dst = latb.at[jnp.where(e["next_passing"], 4, m), rows(q, j)]
                    arrived(src, lat_sem(m, q, j), cond)
                    send(src, dst, lat_sem(m, q, j), dev(dz=e["onward"]), cond)

    def lat_last(q):
        for j in range(2):
            for m in range(4):
                e = route[m]
                cond = jnp.logical_and(e["on"], e["dist"] == e["reach"])
                arrived(latb.at[m, rows(q, j)], lat_sem(m, q, j), cond)

    piece = {}
    for q in range(2):
        for ab in range(2):
            piece[q, ab] = dict(core=rnum.take(), a=rnum.take(3), b=rnum.take(3), g1=rnum.take(3),
                                g2=rnum.take(3), g3=rnum.take())

    def decode(q):
        for ab in range(2):
            def tile(i, _):
                left = jnp.concatenate([latb[m, q * 256 : q * 256 + 256, :] for m in range(4)], axis=1)
                at = pl.multiple_of(ab * 1024 + i * 256, 256)
                part = jnp.dot(left, wp[:, pl.ds(at, 256)], preferred_element_type=F32)
                p32[ab, :, :, :, pl.ds(mul(i, 256), 256)] = part.reshape(2, 2, 64, 256)
                return 0

            lax.fori_loop(0, 4, tile, 0)
            cs[q, ab] = p32[ab, :, o].astype(BF)
            send(cs.at[q, ab], cr.at[q, ab], piece[q, ab]["core"], dev(flip=1))

    def stage_a(q):
        for ab in range(2):
            arrived(cr.at[q, ab], piece[q, ab]["core"])
            total = (p32[ab, :, c] + cr[q, ab].astype(F32)).reshape(4, 2, 16, 1024)
            s32[ab] = total
            ys[q, ab] = total.astype(BF)
            for d in (1, 2, 3):
                sem = piece[q, ab]["a"] + d - 1
                if ab == 0:
                    to = (y + d) % 4
                    src = ys.at[q, 0, :, to // 2, :, pl.ds(mul(to % 2, 512), 512)]
                    send(src, ra.at[q, d - 1], sem, dev(dy=d))
                else:
                    send(ys.at[q, 1, (x + d) % 4], rb.at[q, d - 1], sem, dev(dx=d))

    def stage_b(q):
        for ab in range(2):
            buf = ra if ab == 0 else rb
            for d in (1, 2, 3):
                arrived(buf.at[q, d - 1], piece[q, ab]["a"] + d - 1)
            if ab == 0:
                total = s32[0, :, yh, :, pl.ds(mul(k, 512), 512)]
            else:
                total = s32[1, x]
            for d in range(3):
                total = total + buf[q, d].astype(F32)
            if ab == 0:
                u32[0] = total
                xs[q, 0] = total.astype(BF)
            else:
                for yy in range(4):
                    block = total[yy // 2, :, (yy % 2) * 512 : (yy % 2) * 512 + 512]
                    u32[1, yy] = block
                    xs[q, 1, yy] = block.astype(BF)
            for d in (1, 2, 3):
                sem = piece[q, ab]["b"] + d - 1
                if ab == 0:
                    send(xs.at[q, 0, (x + d) % 4], rx.at[q, 0, d - 1], sem, dev(dx=d))
                else:
                    send(xs.at[q, 1, (y + d) % 4], rx.at[q, 1, d - 1], sem, dev(dy=d))

    def block_of(q, ab, xx, yy):
        cols = pl.ds(pl.multiple_of(ab * 1024 + (yy % 2) * 512, 512), 512)
        return err.at[q, xx // 2, c, xx % 2, yy // 2, :, cols]

    def line_of(q, ab, xx, yy):
        if ab == 0:
            cols = pl.ds(mul(yy % 2, 512), 512)
            return err.at[q, :, c, :, yy // 2, :, cols]
        return err.at[q, xx // 2, c, xx % 2, :, :, 1024:2048]

    def stage_c(q):
        for ab in range(2):
            for d in (1, 2, 3):
                arrived(rx.at[q, ab, d - 1], piece[q, ab]["b"] + d - 1)
            total = u32[ab, x if ab == 0 else y]
            for d in range(3):
                total = total + rx[q, ab, d].astype(F32)
            rc[q, :, ab * 512 : ab * 512 + 512] = total.astype(BF)
            diff = total - tg[q, :, ab * 512 : ab * 512 + 512].astype(F32)
            cols = pl.ds(pl.multiple_of(ab * 1024 + k * 512, 512), 512)
            err[q, x // 2, c, x % 2, yh, :, cols] = diff.astype(BF)
            mine_ = block_of(q, ab, x, y)
            for d in (1, 2, 3):
                to = dev(dx=d) if ab == 0 else dev(dy=d)
                send(mine_, mine_, piece[q, ab]["g1"] + d - 1, to)

    def stage_d(q):
        for ab in range(2):
            for d in (1, 2, 3):
                if ab == 0:
                    block = block_of(q, 0, (x - d + 4) % 4, y)
                else:
                    block = block_of(q, 1, x, (y - d + 4) % 4)
                arrived(block, piece[q, ab]["g1"] + d - 1)
            line = line_of(q, ab, x, y)
            for d in (1, 2, 3):
                to = dev(dy=d) if ab == 0 else dev(dx=d)
                send(line, line, piece[q, ab]["g2"] + d - 1, to)

    def stage_e(q):
        for ab in range(2):
            for d in (1, 2, 3):
                line = line_of(q, ab, (x - d + 4) % 4, (y - d + 4) % 4)
                arrived(line, piece[q, ab]["g2"] + d - 1)
            half = err.at[q, :, c, :, :, :, ab * 1024 : ab * 1024 + 1024]
            send(half, half, piece[q, ab]["g3"], dev(flip=1))

    def stage_f(q):
        for ab in range(2):
            arrived(err.at[q, :, o, :, :, :, ab * 1024 : ab * 1024 + 1024], piece[q, ab]["g3"])

        def one(m, _):
            term[q, m] = lax.dot_general(
                err[q].reshape(256, 2048), wp[pl.ds(mul(m, 256), 256), :],
                (((1,), (1,)), ((), ())), preferred_element_type=F32,
            )
            return 0

        lax.fori_loop(0, 4, one, 0)

    def grad_step(q, depth):
        for j in range(2):
            for m in range(4):
                if depth > (3, 3, 2, 0)[m]:
                    continue
                e = route[m]
                cond = jnp.logical_and(e["on"], e["reach"] - e["dist"] == depth)
                sem = gr_r + m * 4 + q * 2 + j
                r = slice(q * 256 + j * 128, q * 256 + j * 128 + 128)
                tr = slice(j * 128, j * 128 + 128)
                if depth:
                    arrived(gr.at[m, r], sem, cond)

                @pl.when(cond)
                def _():
                    part = term[q, m, tr, :]
                    if depth:
                        part = jnp.where(e["passing"], 0.0, part) + gr[m, r, :].astype(F32)
                    gs[m, r, :] = part.astype(BF)

                last = jnp.logical_and(e["dn"], e["dist"] == 1)
                slot = jnp.where(last, 4, m)
                send(gs.at[m, r], gr.at[slot, r], gr_r + slot * 4 + q * 2 + j, dev(dz=e["back"]), cond)

    def finish(q, j):
        r = slice(q * 256 + j * 128, q * 256 + j * 128 + 128)
        tr = slice(j * 128, j * 128 + 128)
        i = q * 2 + j

        @pl.when(home)
        def _():
            lg[...] = term[q, mine, tr, :]

        arrived(gr.at[mine, r], gr_r + mine * 4 + i, home_up)

        @pl.when(home_up)
        def _():
            lg[...] += gr[mine, r, :].astype(F32)

        arrived(gr.at[4, r], gr_r + 16 + i, home_dn)

        @pl.when(home_dn)
        def _():
            lg[...] += gr[4, r, :].astype(F32)

        @pl.when(home)
        def _():
            grad = lg[...] * gp[r, :]
            pg[r, :] = grad.astype(BF)
            total = jnp.sum(grad, axis=0, keepdims=True)
            if i == 0:
                bs[...] = jnp.broadcast_to(total, (8, 256))
            else:
                bs[...] += jnp.broadcast_to(total, (8, 256))

        send(pg.at[r], pg.at[r], pg_r + i, mate, home)

    def flip_inputs(q, kk):
        def one(i, _):
            block = xp[q, kk, :, :, :, :, pl.ds(mul(i, 256), 256)].reshape(128, 256)
            xt[pl.ds(mul(i, 256), 256), q * 256 + kk * 128 : q * 256 + kk * 128 + 128] = block.T
            return 0

        lax.fori_loop(0, 8, one, 0)

    def flip_latents(q):
        for m in range(4):
            lt[m * 256 : m * 256 + 256, q * 256 : q * 256 + 256] = latb[m, q * 256 : q * 256 + 256, :].T

    dec_copies = {}

    def dec_part(i):
        ab, hh = i // 2, i % 2
        if i >= 2:
            dec_copies[i - 2].wait()

        def tile(t, _):
            at = pl.multiple_of(i * 512 + t * 256, 256)
            right = err[:, :, :, :, :, :, pl.ds(at, 256)].reshape(512, 256)
            out = jnp.dot(lt[...], right, preferred_element_type=F32)
            dg[i % 2, :, pl.ds(mul(t, 256), 256)] = out.astype(BF)
            return 0

        lax.fori_loop(0, 2, tile, 0)
        start = hh * 1024 + ab * 512
        dec_copies[i] = local(dg.at[i % 2], dec_hbm.at[:, start : start + 512])

    lat_relay(0)
    lat_last(0)
    for copy in load_w:
        copy.wait()
    decode(0)
    stage_a(0)
    lat_relay(1)
    flip_latents(0)
    stage_b(0)
    lat_last(1)
    decode(1)
    arrived(tg.at[1 - k], mate_t)
    stage_c(0)
    stage_a(1)
    stage_d(0)
    arrived(xp.at[c, 1 - k], mate_x)
    send(xp.at[c, 1 - k], xp.at[c, 1 - k], core_x, dev(flip=1))
    flip_latents(1)
    stage_b(1)
    stage_e(0)
    stage_c(1)
    arrived(xp.at[o, 1 - k], core_x)
    for q in range(2):
        gp[rows(q, 1), :] = preact(q, 1 - k)[1]
    stage_f(0)
    grad_step(0, 0)
    stage_d(1)
    flip_inputs(0, 0)
    flip_inputs(0, 1)
    stage_e(1)
    grad_step(0, 1)
    flip_inputs(1, 0)
    flip_inputs(1, 1)
    stage_f(1)
    grad_step(1, 0)
    recs[:, pl.ds(mul(k, 1024), 1024)] = rc[k]
    send(rc.at[1 - k], recs.at[:, pl.ds(mul(k, 1024), 1024)], mate_rec, mate)
    grad_step(0, 2)
    dec_part(0)
    grad_step(1, 1)
    grad_step(0, 3)
    dec_part(1)
    grad_step(1, 2)
    dec_part(2)
    finish(0, 0)
    finish(0, 1)
    grad_step(1, 3)
    dec_part(3)
    finish(1, 0)
    finish(1, 1)
    send(bs, bs, mate_bias, mate, home)
    for i in range(4):
        r = slice(i * 128, i * 128 + 128)
        arrived(pg.at[r], pg_r + i, away)

    def enc_tile(i, _):
        r = pl.ds(mul(i, 256), 256)
        encv[r, :] = jnp.dot(xt[r, :], pg[...], preferred_element_type=F32).astype(BF)
        return 0

    lax.fori_loop(0, 8, enc_tile, 0)
    enc_copy = local(encv, enc_hbm)
    arrived(bs, mate_bias, away)
    bias_ref[...] = bs[0:1, :]
    arrived(recs.at[:, pl.ds(mul(1 - k, 1024), 1024)], mate_rec)
    rec_ref[...] = recs[...]
    for copy, cond in late:
        if cond is None:
            copy.wait_send()
        else:
            pl.when(cond)(copy.wait_send)
    dec_copies[2].wait()
    dec_copies[3].wait()
    enc_copy.wait()
    assert snum.count <= 200 and rnum.count <= 120 and lnum.count <= 20, (snum.count, rnum.count)


def shards(layer_inputs, layer_targets, encoder_weight, encoder_bias, decoder_weight):
    vm, hbm = pl.BlockSpec(memory_space=pltpu.VMEM), pl.BlockSpec(memory_space=pl.ANY)
    scratch = [
        pltpu.VMEM((2, 2, 2, 2, 2, 16, 2048), BF),
        pltpu.VMEM((2048, 512), BF),
        pltpu.VMEM((2048, 256), BF),
        pltpu.VMEM((1024, 2048), BF),
        pltpu.VMEM((2, 128, 256), BF),
        pltpu.VMEM((5, 512, 256), BF),
        pltpu.VMEM((1024, 512), BF),
        pltpu.VMEM((512, 256), F32),
        pltpu.VMEM((2, 16, 1024), BF),
        pltpu.VMEM((2, 2, 2, 64, 1024), F32),
        pltpu.VMEM((2, 2, 2, 64, 1024), BF),
        pltpu.VMEM((2, 2, 2, 64, 1024), BF),
        pltpu.VMEM((2, 4, 2, 16, 1024), F32),
        pltpu.VMEM((2, 2, 4, 2, 16, 1024), BF),
        pltpu.VMEM((2, 3, 4, 16, 512), BF),
        pltpu.VMEM((2, 3, 2, 16, 1024), BF),
        pltpu.VMEM((2, 4, 16, 512), F32),
        pltpu.VMEM((2, 2, 4, 16, 512), BF),
        pltpu.VMEM((2, 2, 3, 16, 512), BF),
        pltpu.VMEM((2, 16, 1024), BF),
        pltpu.VMEM((2, 2, 2, 2, 2, 16, 2048), BF),
        pltpu.VMEM((2, 4, 256, 256), F32),
        pltpu.VMEM((5, 512, 256), BF),
        pltpu.VMEM((4, 512, 256), BF),
        pltpu.VMEM((128, 256), F32),
        pltpu.VMEM((512, 256), BF),
        pltpu.VMEM((8, 256), F32),
        pltpu.VMEM((16, 2048), BF),
        pltpu.VMEM((2048, 256), BF),
        pltpu.VMEM((2, 1024, 512), BF),
        pltpu.SemaphoreType.DMA((200,)),
        pltpu.SemaphoreType.DMA((120,)),
        pltpu.SemaphoreType.DMA((20,)),
    ]
    rec, enc, bias, dec = pl.pallas_call(
        kernel,
        out_shape=(
            jax.ShapeDtypeStruct((16, 2048), BF),
            jax.ShapeDtypeStruct((2048, 256), BF),
            jax.ShapeDtypeStruct((1, 256), F32),
            jax.ShapeDtypeStruct((1024, 2048), BF),
        ),
        in_specs=[hbm, vm, hbm, vm, hbm],
        out_specs=(vm, hbm, vm, hbm),
        scratch_shapes=scratch,
        compiler_params=pltpu.CompilerParams(
            collective_id=0, has_side_effects=True, vmem_limit_bytes=56 * 1024 * 1024
        ),
        name="transcoder_step",
    )(
        layer_inputs.reshape(2, 2, 2, 2, 16, 2048),
        layer_targets[0],
        encoder_weight[0],
        encoder_bias,
        decoder_weight.reshape(1024, 2048),
    )
    return rec[None], enc[None], bias, dec.reshape(1, 4, 1, 256, 2048)


def solution(mesh):
    placed = (
        P("layer", "tok", None),
        P("layer", ("latent", "tok"), None),
        P("layer", None, "latent"),
        P("layer", "latent"),
        P("layer", None, "tok", "latent", None),
    )
    return jax.shard_map(
        shards,
        mesh=mesh,
        in_specs=placed,
        out_specs=(
            P("layer", ("latent", "tok"), None),
            P("layer", None, "latent"),
            P("layer", "latent"),
            P("layer", None, "tok", "latent", None),
        ),
        check_vma=False,
    )
```

```python
import jax
import jax.numpy as jnp
from jax import lax
from jax.experimental import pallas as pl
from jax.experimental.pallas import tpu as pltpu
from jax.sharding import PartitionSpec as P

MESH = pl.DeviceIdType.MESH
SPLIT = 2
SUB = 128 // SPLIT
COUNTS = (47, 109, 12)
BF = jnp.bfloat16
F32 = jnp.float32


def mul(value, by):
    return pl.multiple_of(value * by, by)


class Numbers:
    def __init__(self):
        self.count = 0

    def take(self, n=1):
        base = self.count
        self.count += n
        return base


def kernel(
    x_hbm, t_hbm, we_hbm, b_hbm, w_hbm,
    rec_hbm, bias_hbm, pg_hbm, xt_hbm, dec_hbm,
    t_ref, b_ref,    xp, xt, we, wp, own, latb, lt, gp, tg, p32, cs, cr, s32, ys, ra, rb, u32, xs, rx, rc, err,
    term, gr, gs, lg, pg, bs, recs, dg, ss, rs, ls,
):
    z, lat, k = lax.axis_index("layer"), lax.axis_index("latent"), lax.axis_index("tok")
    x, yh, c = lat // 4, (lat // 2) % 2, lat % 2
    y = yh * 2 + k
    h = z % 2
    o = 1 - c

    def dev(dx=0, dy=0, dz=0, flip=0):
        xx, yy, zz = (x + dx) % 4, (y + dy) % 4, (z + dz) % 8
        cc = o if flip else c
        return (zz, xx * 4 + (yy // 2) * 2 + cc, yy % 2)

    mate = (z, lat, 1 - k)
    snum, rnum, lnum = Numbers(), Numbers(), Numbers()
    sent = []

    def rc_(src, dst, si, ri, to):
        return pltpu.make_async_remote_copy(
            src_ref=src, dst_ref=dst, send_sem=ss.at[si], recv_sem=rs.at[ri],
            device_id=to, device_id_type=MESH,
        )

    def group(like, cond=None):
        si = snum.take()
        sent.append((si, like, cond))
        return si

    def send(src, dst, si, ri, to, cond=None):
        copy = rc_(src, dst, si, ri, to)
        if cond is None:
            copy.start()
        else:
            pl.when(cond)(copy.start)

    def arrived(dst, ri, cond=None):
        copy = rc_(dst, dst, 0, ri, mate)
        if cond is None:
            copy.wait_recv()
        else:
            pl.when(cond)(copy.wait_recv)

    def local(src, dst, li=None):
        copy = pltpu.make_async_copy(src, dst, ls.at[lnum.take() if li is None else li])
        copy.start()
        return copy

    def landed(dst, li):
        pltpu.make_async_copy(dst, dst, ls.at[li]).wait()

    load_x = [lnum.take(), lnum.take()]
    for cc in range(2):
        local(x_hbm.at[:, :, cc, 0], xp.at[0, k, cc], load_x[0])
    load_we = local(we_hbm, we)
    load_b = local(b_hbm, b_ref)
    for cc in range(2):
        local(x_hbm.at[:, :, cc, 1], xp.at[1, k, cc], load_x[1])

    load_t = local(t_hbm, t_ref)

    barrier = pltpu.get_barrier_semaphore()
    peers = [dev(dz=1), dev(dz=-1), dev(flip=1)]
    peers += [dev(dy=d) for d in (1, 2, 3)] + [dev(dx=d) for d in (1, 2, 3)]
    for to in peers:
        pl.semaphore_signal(barrier, inc=1, device_id=to, device_id_type=MESH)

    ku = [4, 4, 3 - k, 1 - k]
    kd = [3, 3 * (1 - k), 0, 0]
    route = []
    for m in range(4):
        s = 2 * m + k
        u, d = z - s, (s - z + 8) % 8
        on_up = jnp.logical_and(u >= 1, u <= ku[m])
        on_dn = jnp.logical_and(d >= 1, d <= kd[m])
        on = jnp.logical_or(on_up, on_dn)
        dist = jnp.where(on_up, u, d)
        reach = jnp.where(on_up, ku[m], kd[m])
        passing = jnp.logical_and(on_dn, z < s)
        next_passing = jnp.logical_and(on_dn, (z + 7) % 8 < s)
        next_passing = jnp.logical_and(next_passing, z > 0)
        route.append(dict(on=on, up=on_up, dn=on_dn, dist=dist, reach=reach, passing=passing,
                          next_passing=next_passing, valid=s <= z,
                          onward=jnp.where(on_up, 1, 7), back=jnp.where(on_up, 7, 1)))
    mine = z // 2
    home = k == h
    ku_own = jnp.where(mine == 0, 4, jnp.where(mine == 1, 4, jnp.where(mine == 2, 3 - k, 1 - k)))
    kd_own = jnp.where(mine == 0, 3, jnp.where(mine == 1, 3 * (1 - k), 0))
    home_up = jnp.logical_and(home, ku_own > 0)
    home_dn = jnp.logical_and(home, kd_own > 0)
    away = jnp.logical_not(home)

    def clear():
        for m in range(4):
            @pl.when(jnp.logical_not(route[m]["valid"]))
            def _():
                latb[m] = jnp.zeros((512, 256), BF)

    lat_r = rnum.take(16 * SPLIT)
    mate_x, core_x, mate_t, mate_rec, mate_bias = (rnum.take() for _ in range(5))
    pg_r = rnum.take(4 * SPLIT)
    gr_r = rnum.take(20 * SPLIT)

    def lat_sem(m, q, j):
        return lat_r + m * (4 * SPLIT) + q * (2 * SPLIT) + j

    def rows(q, j):
        kk = k if j == 0 else 1 - k
        return pl.ds(pl.multiple_of(q * 256 + kk * 128, 128), 128)

    def some(q, j):
        kk = k if j < SPLIT else 1 - k
        return pl.ds(pl.multiple_of(q * 256 + kk * 128 + (j % SPLIT) * SUB, SUB), SUB)

    up_si, dn_si = group(latb.at[0], home_up), group(latb.at[0], home_dn)
    away_si, pg_si = group(own, away), group(pg, home)
    lat_si = [[snum.take() for m in range(3)] for q in range(2)]
    gr_si = [[snum.take() for m in range(4)] for q in range(2)]

    def origin_send(q, j):
        r = some(q, j)
        src = latb.at[mine, r]
        send(src, src, up_si, lat_sem(mine, q, j), dev(dz=1), home_up)
        slot = jnp.where(z >= 1, 4, mine)
        send(src, latb.at[slot, r], dn_si, lat_sem(mine, q, j), dev(dz=-1), home_dn)

    def gate(v):
        inner = 0.7978845608028654 * (v + 0.044715 * (v * v * v))
        t = jnp.tanh(inner)
        cdf = 0.5 * (1.0 + t)
        slope = cdf + 0.5 * v * (1.0 - t * t) * (0.7978845608028654 * (1.0 + 0.134145 * (v * v)))
        return v * cdf, slope

    def preact(q, kk):
        v = jnp.dot(xp[q, kk].reshape(128, 2048), we[...], preferred_element_type=F32) + b_ref[...]
        return gate(v)

    def encode(q):
        landed(xp.at[q, k], load_x[q])
        val, slope = preact(q, k)
        val = val.astype(BF)
        own[q] = val
        gp[rows(q, 0), :] = slope

        @pl.when(home)
        def _():
            latb[mine, rows(q, 0), :] = val

    def first_send(q):
        for j in range(SPLIT):
            src = own.at[q, j * SUB : j * SUB + SUB]
            send(src, latb.at[mine, some(q, j)], away_si, lat_sem(mine, q, SPLIT + j), mate, away)
            origin_send(q, j)

    def send_inputs():
        load_t.wait()
        tg[k] = t_ref[:, pl.ds(mul(k, 1024), 1024)]
        send(t_ref.at[:, pl.ds(mul(1 - k, 1024), 1024)], tg.at[k], group(tg.at[k]), mate_t, mate)
        send(xp.at[c, k], xp.at[c, k], group(xp.at[c, k]), mate_x, mate)

    def lat_hop(q, far):
        if far == 0:
            for j in range(SPLIT, 2 * SPLIT):
                arrived(latb.at[mine, some(q, j)], lat_sem(mine, q, j), home)
                origin_send(q, j)
            return
        conds = []
        for m in range(3):
            e = route[m]
            cond = jnp.logical_and(e["on"], jnp.logical_and(e["dist"] == far, e["dist"] < e["reach"]))
            conds.append(cond)
            if not (far == 3 and m == 2):
                sent.append((lat_si[q][m], latb.at[0, 0:256], cond))
        for kk in range(2):
            for m in range(3):
                if far == 3 and m == 2:
                    continue
                e = route[m]

                @pl.when(conds[m])
                def _():
                    for j in range(kk * SPLIT, kk * SPLIT + SPLIT):
                        src = latb.at[jnp.where(e["passing"], 4, m), some(q, j)]
                        dst = latb.at[jnp.where(e["next_passing"], 4, m), some(q, j)]
                        arrived(src, lat_sem(m, q, j))
                        send(src, dst, lat_si[q][m], lat_sem(m, q, j), dev(dz=e["onward"]))

    def lat_last(q):
        for m in range(4):
            e = route[m]

            @pl.when(jnp.logical_and(e["on"], e["dist"] == e["reach"]))
            def _():
                for j in range(2 * SPLIT):
                    arrived(latb.at[m, some(q, j)], lat_sem(m, q, j))

    piece = {}
    for q in range(2):
        for ab in range(2):
            piece[q, ab] = {name: rnum.take() for name in ("core", "a", "b", "g1", "g2", "g3")}

    def decode(q, ab):
        left = jnp.concatenate([latb[m, q * 256 : q * 256 + 256, :] for m in range(4)], axis=1)
        part = jnp.dot(left, wp[:, ab * 1024 : ab * 1024 + 1024], preferred_element_type=F32)
        p32[ab] = part.reshape(2, 2, 64, 1024)
        cs[q, ab] = p32[ab, :, o].astype(BF)
        send(cs.at[q, ab], cr.at[q, ab], group(cs.at[q, ab]), piece[q, ab]["core"], dev(flip=1))

    def stage_a(q):
        for ab in range(2):
            arrived(cr.at[q, ab], piece[q, ab]["core"])
            total = (p32[ab, :, c] + cr[q, ab].astype(F32)).reshape(4, 2, 16, 1024)
            s32[ab] = total
            ys[q, ab] = total.astype(BF)
            wide = ra.at[q] if ab == 0 else rb.at[q]
            si, sem = group(wide), piece[q, ab]["a"]
            for d in (1, 2, 3):
                if ab == 0:
                    to = (y + d) % 4
                    src = ys.at[q, 0, :, to // 2, :, pl.ds(mul(to % 2, 512), 512)]
                    send(src, ra.at[q, d - 1], si, sem, dev(dy=d))
                else:
                    send(ys.at[q, 1, (x + d) % 4], rb.at[q, d - 1], si, sem, dev(dx=d))

    def stage_b(q):
        for ab in range(2):
            buf = ra if ab == 0 else rb
            arrived(buf.at[q], piece[q, ab]["a"])
            if ab == 0:
                total = s32[0, :, yh, :, pl.ds(mul(k, 512), 512)]
            else:
                total = s32[1, x]
            for d in range(3):
                total = total + buf[q, d].astype(F32)
            if ab == 0:
                u32[0] = total
                xs[q, 0] = total.astype(BF)
            else:
                for yy in range(4):
                    block = total[yy // 2, :, (yy % 2) * 512 : (yy % 2) * 512 + 512]
                    u32[1, yy] = block
                    xs[q, 1, yy] = block.astype(BF)
            si, sem = group(rx.at[q, ab]), piece[q, ab]["b"]
            for d in (1, 2, 3):
                if ab == 0:
                    send(xs.at[q, 0, (x + d) % 4], rx.at[q, 0, d - 1], si, sem, dev(dx=d))
                else:
                    send(xs.at[q, 1, (y + d) % 4], rx.at[q, 1, d - 1], si, sem, dev(dy=d))

    def block_of(q, ab, xx, yy):
        cols = pl.ds(pl.multiple_of(ab * 1024 + (yy % 2) * 512, 512), 512)
        return err.at[q, xx // 2, c, xx % 2, yy // 2, :, cols]

    def line_of(q, ab, xx, yy):
        if ab == 0:
            cols = pl.ds(mul(yy % 2, 512), 512)
            return err.at[q, :, c, :, yy // 2, :, cols]
        return err.at[q, xx // 2, c, xx % 2, :, :, 1024:2048]

    def stage_c(q):
        for ab in range(2):
            arrived(rx.at[q, ab], piece[q, ab]["b"])
            total = u32[ab, x if ab == 0 else y]
            for d in range(3):
                total = total + rx[q, ab, d].astype(F32)
            rc[q, :, ab * 512 : ab * 512 + 512] = total.astype(BF)
            diff = total - tg[q, :, ab * 512 : ab * 512 + 512].astype(F32)
            cols = pl.ds(pl.multiple_of(ab * 1024 + k * 512, 512), 512)
            err[q, x // 2, c, x % 2, yh, :, cols] = diff.astype(BF)
            mine_ = block_of(q, ab, x, y)
            si = group(rx.at[q, ab])
            for d in (1, 2, 3):
                to = dev(dx=d) if ab == 0 else dev(dy=d)
                send(mine_, mine_, si, piece[q, ab]["g1"], to)

    def stage_d(q):
        for ab in range(2):
            arrived(rx.at[q, ab], piece[q, ab]["g1"])
            line = line_of(q, ab, x, y)
            si = group(ra.at[q])
            for d in (1, 2, 3):
                to = dev(dy=d) if ab == 0 else dev(dx=d)
                send(line, line, si, piece[q, ab]["g2"], to)

    def stage_e(q):
        for ab in range(2):
            arrived(ra.at[q], piece[q, ab]["g2"])
            half = err.at[q, :, c, :, :, :, ab * 1024 : ab * 1024 + 1024]
            send(half, half, group(half), piece[q, ab]["g3"], dev(flip=1))

    def stage_f(q):
        for ab in range(2):
            arrived(err.at[q, :, o, :, :, :, ab * 1024 : ab * 1024 + 1024], piece[q, ab]["g3"])

        for half in range(2):
            out = lax.dot_general(
                err[q].reshape(256, 2048), wp[half * 512 : half * 512 + 512, :],
                (((1,), (1,)), ((), ())), preferred_element_type=F32,
            )
            term[q, 2 * half] = out[:, :256]
            term[q, 2 * half + 1] = out[:, 256:]

    def grad_step(q, depth):
        for m in range(4):
            if depth > (3, 3, 2, 0)[m]:
                continue
            e = route[m]
            cond = jnp.logical_and(e["on"], e["reach"] - e["dist"] == depth)
            sent.append((gr_si[q][m], latb.at[0, 0:256], cond))

            @pl.when(cond)
            def _():
                slot = jnp.where(jnp.logical_and(e["dn"], e["dist"] == 1), 4, m)
                for j in range(2 * SPLIT):
                    sem = gr_r + m * (4 * SPLIT) + q * (2 * SPLIT) + j
                    r = slice(q * 256 + j * SUB, q * 256 + j * SUB + SUB)
                    part = term[q, m, j * SUB : j * SUB + SUB, :]
                    if depth:
                        arrived(gr.at[m, r], sem)
                        part = jnp.where(e["passing"], 0.0, part) + gr[m, r, :].astype(F32)
                    gs[m, r, :] = part.astype(BF)
                    sem = gr_r + slot * (4 * SPLIT) + q * (2 * SPLIT) + j
                    send(gs.at[m, r], gr.at[slot, r], gr_si[q][m], sem, dev(dz=e["back"]))

    def finish(q):
        for j in range(2 * SPLIT):
            i = q * 2 * SPLIT + j
            r = slice(i * SUB, i * SUB + SUB)

            @pl.when(home)
            def _():
                lg[...] = term[q, mine, j * SUB : j * SUB + SUB, :]

            @pl.when(home_up)
            def _():
                arrived(gr.at[mine, r], gr_r + mine * (4 * SPLIT) + i)
                lg[...] += gr[mine, r, :].astype(F32)

            @pl.when(home_dn)
            def _():
                arrived(gr.at[4, r], gr_r + 16 * SPLIT + i)
                lg[...] += gr[4, r, :].astype(F32)

            @pl.when(home)
            def _():
                grad = lg[...] * gp[r, :]
                pg[r, :] = grad.astype(BF)
                total = jnp.sum(grad, axis=0, keepdims=True)
                if i == 0:
                    bs[...] = jnp.broadcast_to(total, (8, 256))
                else:
                    bs[...] += jnp.broadcast_to(total, (8, 256))
                send(pg.at[r], pg.at[r], pg_si, pg_r + i, mate)

    def flip_inputs(q, j):
        kk = k if j == 0 else 1 - k
        for i in range(2):
            block = xp[q, kk, :, :, :, :, i * 1024 : i * 1024 + 1024].reshape(128, 1024)
            xt[i * 1024 : i * 1024 + 1024, rows(q, j)] = block.T

    def flip_latents(q):
        for m in range(4):
            lt[m * 256 : m * 256 + 256, q * 256 : q * 256 + 256] = latb[m, q * 256 : q * 256 + 256, :].T

    dec_copies, dec_sem = {}, [lnum.take(), lnum.take()]

    def dec_part(i):
        ab, hh = i // 2, i % 2
        if i >= 2:
            dec_copies[i - 2].wait()

        right = err[:, :, :, :, :, :, i * 512 : i * 512 + 512].reshape(512, 512)
        dg[i % 2] = jnp.dot(lt[...], right, preferred_element_type=F32).astype(BF)
        start = hh * 1024 + ab * 512
        dec_copies[i] = local(dg.at[i % 2], dec_hbm.at[:, start : start + 512], dec_sem[i % 2])

    load_we.wait()
    load_b.wait()
    encode(0)
    pl.semaphore_wait(barrier, len(peers))
    first_send(0)
    encode(1)
    load_w = lnum.take()
    for ab in range(2):
        for hh in range(2):
            local(
                w_hbm.at[:, hh * 1024 + ab * 512 : hh * 1024 + ab * 512 + 512],
                wp.at[:, ab * 1024 + hh * 512 : ab * 1024 + hh * 512 + 512],
                load_w,
            )
    clear()
    lat_hop(0, 0)
    lat_hop(0, 1)
    first_send(1)
    send_inputs()
    flip_inputs(0, 0)
    lat_hop(0, 2)
    lat_hop(1, 0)
    lat_hop(1, 1)
    lat_hop(0, 3)
    flip_inputs(1, 0)
    lat_hop(1, 2)
    lat_last(0)
    landed(wp, load_w)
    decode(0, 0)
    lat_hop(1, 3)
    decode(0, 1)
    stage_a(0)
    flip_latents(0)
    lat_last(1)
    decode(1, 0)
    decode(1, 1)
    stage_b(0)
    flip_latents(1)
    stage_a(1)
    arrived(tg.at[1 - k], mate_t)
    stage_c(0)
    stage_b(1)
    arrived(xp.at[c, 1 - k], mate_x)
    send(xp.at[c, 1 - k], xp.at[c, 1 - k], group(xp.at[c, 1 - k]), core_x, dev(flip=1))
    stage_d(0)
    stage_c(1)
    stage_e(0)
    arrived(xp.at[o, 1 - k], core_x)
    for q in range(2):
        gp[rows(q, 1), :] = preact(q, 1 - k)[1]
    flip_inputs(0, 1)
    stage_d(1)
    stage_f(0)
    grad_step(0, 0)
    flip_inputs(1, 1)
    xt_copy = local(xt, xt_hbm)
    recs[:, pl.ds(mul(k, 1024), 1024)] = rc[k]
    send(rc.at[1 - k], recs.at[:, pl.ds(mul(k, 1024), 1024)], group(rc.at[1 - k]), mate_rec, mate)
    grad_step(0, 1)
    stage_e(1)
    grad_step(0, 2)
    stage_f(1)
    grad_step(1, 0)
    grad_step(0, 3)
    dec_part(0)
    grad_step(1, 1)
    finish(0)
    dec_part(1)
    grad_step(1, 2)
    dec_part(2)
    grad_step(1, 3)
    dec_part(3)
    finish(1)
    send(bs, bs, group(bs, home), mate_bias, mate, home)
    for i in range(4 * SPLIT):
        arrived(pg.at[i * SUB : i * SUB + SUB], pg_r + i, away)

    pg_copy = local(pg, pg_hbm)
    arrived(bs, mate_bias, away)
    bias_copy = local(bs.at[0:1], bias_hbm)
    arrived(recs.at[:, pl.ds(mul(1 - k, 1024), 1024)], mate_rec)
    rec_copy = local(recs, rec_hbm)
    for si, like, cond in sent:
        copy = rc_(like, like, si, 0, mate)
        if cond is None:
            copy.wait_send()
        else:
            pl.when(cond)(copy.wait_send)
    dec_copies[2].wait()
    dec_copies[3].wait()
    for copy in (xt_copy, pg_copy, bias_copy, rec_copy):
        copy.wait()
    assert (snum.count, rnum.count, lnum.count) == COUNTS, (snum.count, rnum.count, lnum.count)


def outputs(rec_in, bias_in, pg_hbm, xt_hbm, dec_in, rec, enc, bias, dec, recv, biasv, pg, xt, encv, decv, sem):
    def part(i):
        return pl.ds(i * 256, 256)

    loads = [pltpu.make_async_copy(pg_hbm, pg, sem.at[0]), pltpu.make_async_copy(xt_hbm, xt, sem.at[1])]
    dec_loads = [pltpu.make_async_copy(dec_in.at[part(i)], decv.at[part(i)], sem.at[2 + i]) for i in range(4)]
    dec_stores = [pltpu.make_async_copy(decv.at[part(i)], dec.at[part(i)], sem.at[6 + i]) for i in range(4)]
    enc_store = pltpu.make_async_copy(encv, enc, sem.at[10])
    small_loads = [pltpu.make_async_copy(rec_in, recv, sem.at[11]), pltpu.make_async_copy(bias_in, biasv, sem.at[12])]
    small_stores = [pltpu.make_async_copy(recv, rec, sem.at[13]), pltpu.make_async_copy(biasv, bias, sem.at[14])]
    for copy in loads + dec_loads + small_loads:
        copy.start()
    for copy in loads:
        copy.wait()
    for i in range(2):
        dec_loads[i].wait()
        dec_stores[i].start()
    encv[...] = jnp.dot(xt[...], pg[...], preferred_element_type=F32).astype(BF)
    enc_store.start()
    for i in range(2, 4):
        dec_loads[i].wait()
        dec_stores[i].start()
    for load, store in zip(small_loads, small_stores):
        load.wait()
        store.start()
    for copy in dec_stores + small_stores + [enc_store]:
        copy.wait()


def kernel1(layer_inputs, layer_targets, encoder_weight, encoder_bias, decoder_weight):
    vm, hbm = pl.BlockSpec(memory_space=pltpu.VMEM), pl.BlockSpec(memory_space=pl.ANY)
    scratch = [
        pltpu.VMEM((16, 2048), BF),
        pltpu.VMEM((1, 256), F32),
        pltpu.VMEM((2, 2, 2, 2, 2, 16, 2048), BF),
        pltpu.VMEM((2048, 512), BF),
        pltpu.VMEM((2048, 256), BF),
        pltpu.VMEM((1024, 2048), BF),
        pltpu.VMEM((2, 128, 256), BF),
        pltpu.VMEM((5, 512, 256), BF),
        pltpu.VMEM((1024, 512), BF),
        pltpu.VMEM((512, 256), F32),
        pltpu.VMEM((2, 16, 1024), BF),
        pltpu.VMEM((2, 2, 2, 64, 1024), F32),
        pltpu.VMEM((2, 2, 2, 64, 1024), BF),
        pltpu.VMEM((2, 2, 2, 64, 1024), BF),
        pltpu.VMEM((2, 4, 2, 16, 1024), F32),
        pltpu.VMEM((2, 2, 4, 2, 16, 1024), BF),
        pltpu.VMEM((2, 3, 4, 16, 512), BF),
        pltpu.VMEM((2, 3, 2, 16, 1024), BF),
        pltpu.VMEM((2, 4, 16, 512), F32),
        pltpu.VMEM((2, 2, 4, 16, 512), BF),
        pltpu.VMEM((2, 2, 3, 16, 512), BF),
        pltpu.VMEM((2, 16, 1024), BF),
        pltpu.VMEM((2, 2, 2, 2, 2, 16, 2048), BF),
        pltpu.VMEM((2, 4, 256, 256), F32),
        pltpu.VMEM((5, 512, 256), BF),
        pltpu.VMEM((4, 512, 256), BF),
        pltpu.VMEM((SUB, 256), F32),
        pltpu.VMEM((512, 256), BF),
        pltpu.VMEM((8, 256), F32),
        pltpu.VMEM((16, 2048), BF),
        pltpu.VMEM((2, 1024, 512), BF),
        *[pltpu.SemaphoreType.DMA((n,)) for n in COUNTS],
    ]
    rec, bias, pg, xt, dec = pl.pallas_call(
        kernel,
        out_shape=(
            jax.ShapeDtypeStruct((16, 2048), BF),
            jax.ShapeDtypeStruct((1, 256), F32),
            jax.ShapeDtypeStruct((512, 256), BF),
            jax.ShapeDtypeStruct((2048, 512), BF),
            jax.ShapeDtypeStruct((1024, 2048), BF),
        ),
        in_specs=[hbm] * 5,
        out_specs=[hbm] * 5,
        scratch_shapes=scratch,
        compiler_params=pltpu.CompilerParams(
            collective_id=0, has_side_effects=True, vmem_limit_bytes=56 * 1024 * 1024
        ),
        name="transcoder_step",
    )(
        layer_inputs.reshape(2, 2, 2, 2, 16, 2048),
        layer_targets[0],
        encoder_weight[0],
        encoder_bias,
        decoder_weight.reshape(1024, 2048),
    )
    return rec, bias, pg, xt, dec


def shards(*args):
    vm, hbm = pl.BlockSpec(memory_space=pltpu.VMEM), pl.BlockSpec(memory_space=pl.ANY)
    rec, bias, pg, xt, dec = kernel1(*args)
    rec, enc, bias, dec = pl.pallas_call(
        outputs,
        out_shape=(
            jax.ShapeDtypeStruct((16, 2048), BF),
            jax.ShapeDtypeStruct((2048, 256), BF),
            jax.ShapeDtypeStruct((1, 256), F32),
            jax.ShapeDtypeStruct((1024, 2048), BF),
        ),
        in_specs=[hbm] * 5,
        out_specs=[hbm] * 4,
        scratch_shapes=[
            pltpu.VMEM((16, 2048), BF),
            pltpu.VMEM((1, 256), F32),
            pltpu.VMEM((512, 256), BF),
            pltpu.VMEM((2048, 512), BF),
            pltpu.VMEM((2048, 256), BF),
            pltpu.VMEM((1024, 2048), BF),
            pltpu.SemaphoreType.DMA((15,)),
        ],
        compiler_params=pltpu.CompilerParams(vmem_limit_bytes=56 * 1024 * 1024),
        name="write_outputs",
    )(rec, bias, pg, xt, dec)
    return rec[None], enc[None], bias, dec.reshape(1, 4, 1, 256, 2048)


def solution(mesh):
    placed = (
        P("layer", "tok", None),
        P("layer", ("latent", "tok"), None),
        P("layer", None, "latent"),
        P("layer", "latent"),
        P("layer", None, "tok", "latent", None),
    )
    return jax.shard_map(
        shards,
        mesh=mesh,
        in_specs=placed,
        out_specs=(
            P("layer", ("latent", "tok"), None),
            P("layer", None, "latent"),
            P("layer", "latent"),
            P("layer", None, "tok", "latent", None),
        ),
        check_vma=False,
    )
```

```python
import jax
import jax.numpy as jnp
from jax import lax
from jax.experimental import pallas as pl
from jax.experimental.pallas import tpu as pltpu
from jax.sharding import PartitionSpec as P

MESH = pl.DeviceIdType.MESH
SPLIT = 2
SUB = 128 // SPLIT
COUNTS = (45, 113, 12)
BF = jnp.bfloat16
F32 = jnp.float32


def mul(value, by):
    return pl.multiple_of(value * by, by)


class Numbers:
    def __init__(self):
        self.count = 0

    def take(self, n=1):
        base = self.count
        self.count += n
        return base


def kernel(
    x_hbm, t_hbm, we_hbm, b_hbm, w_hbm,
    rec_hbm, bias_hbm, pg_hbm, xt_hbm, dec_hbm,
    t_ref, b_ref,    xp, xt, we, wp, own, latb, lt, gp, tg, p32, cs, cr, s32, ys, ra, rb, u32, xs, rx, rc, err,
    term, gr, gs, lg, pg, bs, recs, dg, ss, rs, ls,
):
    z, lat, k = lax.axis_index("layer"), lax.axis_index("latent"), lax.axis_index("tok")
    x, yh, c = lat // 4, (lat // 2) % 2, lat % 2
    y = yh * 2 + k
    h = z % 2
    o = 1 - c

    def dev(dx=0, dy=0, dz=0, flip=0):
        xx, yy, zz = (x + dx) % 4, (y + dy) % 4, (z + dz) % 8
        cc = o if flip else c
        return (zz, xx * 4 + (yy // 2) * 2 + cc, yy % 2)

    mate = (z, lat, 1 - k)
    snum, rnum, lnum = Numbers(), Numbers(), Numbers()
    sent = []

    def rc_(src, dst, si, ri, to):
        return pltpu.make_async_remote_copy(
            src_ref=src, dst_ref=dst, send_sem=ss.at[si], recv_sem=rs.at[ri],
            device_id=to, device_id_type=MESH,
        )

    def group(like, cond=None):
        si = snum.take()
        sent.append((si, like, cond))
        return si

    def send(src, dst, si, ri, to, cond=None):
        copy = rc_(src, dst, si, ri, to)
        if cond is None:
            copy.start()
        else:
            pl.when(cond)(copy.start)

    def arrived(dst, ri, cond=None):
        copy = rc_(dst, dst, 0, ri, mate)
        if cond is None:
            copy.wait_recv()
        else:
            pl.when(cond)(copy.wait_recv)

    def local(src, dst, li=None):
        copy = pltpu.make_async_copy(src, dst, ls.at[lnum.take() if li is None else li])
        copy.start()
        return copy

    def landed(dst, li):
        pltpu.make_async_copy(dst, dst, ls.at[li]).wait()

    load_x = [lnum.take(), lnum.take()]
    for cc in range(2):
        local(x_hbm.at[:, :, cc, 0], xp.at[0, k, cc], load_x[0])
    load_we = local(we_hbm, we)
    load_b = local(b_hbm, b_ref)
    for cc in range(2):
        local(x_hbm.at[:, :, cc, 1], xp.at[1, k, cc], load_x[1])

    load_t = local(t_hbm, t_ref)

    barrier = pltpu.get_barrier_semaphore()
    peers = [dev(dz=1), dev(dz=-1), dev(flip=1)]
    peers += [dev(dy=d) for d in (1, 2, 3)] + [dev(dx=d) for d in (1, 2, 3)]
    across = [((z + 1) % 8, lat, 1 - k), ((z + 7) % 8, lat, 1 - k)]
    across_x = [(z, (x + d) % 4 * 4 + yh * 2 + c, 1 - k) for d in (1, 2, 3)]
    peers += across + across_x
    for to in peers:
        pl.semaphore_signal(barrier, inc=1, device_id=to, device_id_type=MESH)

    ku = [4, 4, 3 - k, 1 - k]
    kd = [3, 3 * (1 - k), 0, 0]
    route = []
    for m in range(4):
        s = 2 * m + k
        u, d = z - s, (s - z + 8) % 8
        on_up = jnp.logical_and(u >= 1, u <= ku[m])
        on_dn = jnp.logical_and(d >= 1, d <= kd[m])
        on = jnp.logical_or(on_up, on_dn)
        dist = jnp.where(on_up, u, d)
        reach = jnp.where(on_up, ku[m], kd[m])
        passing = jnp.logical_and(on_dn, z < s)
        next_passing = jnp.logical_and(on_dn, (z + 7) % 8 < s)
        next_passing = jnp.logical_and(next_passing, z > 0)
        route.append(dict(on=on, up=on_up, dn=on_dn, dist=dist, reach=reach, passing=passing,
                          next_passing=next_passing, valid=s <= z,
                          onward=jnp.where(on_up, 1, 7), back=jnp.where(on_up, 7, 1)))
    mine = z // 2
    home = k == h
    ku_own = jnp.where(mine == 0, 4, jnp.where(mine == 1, 4, jnp.where(mine == 2, 3 - h, 1 - h)))
    kd_own = jnp.where(mine == 0, 3, jnp.where(mine == 1, 3 * (1 - h), 0))
    home_up = jnp.logical_and(home, ku_own > 0)
    home_dn = jnp.logical_and(home, kd_own > 0)
    away = jnp.logical_not(home)
    away_up = jnp.logical_and(away, ku_own > 0)
    away_dn = jnp.logical_and(away, kd_own > 0)

    def clear():
        for m in range(4):
            @pl.when(jnp.logical_not(route[m]["valid"]))
            def _():
                latb[m] = jnp.zeros((512, 256), BF)

    lat_r = rnum.take(16 * SPLIT)
    mate_x, core_x, mate_t, mate_rec, mate_bias = (rnum.take() for _ in range(5))
    pg_r = rnum.take(4 * SPLIT)
    gr_r = rnum.take(20 * SPLIT)

    def lat_sem(m, q, j):
        return lat_r + m * (4 * SPLIT) + q * (2 * SPLIT) + j

    def rows(q, j):
        kk = k if j == 0 else 1 - k
        return pl.ds(pl.multiple_of(q * 256 + kk * 128, 128), 128)

    def some(q, j):
        kk = k if j < SPLIT else 1 - k
        return pl.ds(pl.multiple_of(q * 256 + kk * 128 + (j % SPLIT) * SUB, SUB), SUB)

    up_si, dn_si = group(own, home_up), group(own, home_dn)
    away_si, pg_si = group(own, away), group(pg, home)
    away_up_si, away_dn_si = group(own, away_up), group(own, away_dn)
    lat_si = [[snum.take() for m in range(3)] for q in range(2)]
    gr_si = [[snum.take() for m in range(4)] for q in range(2)]

    def origin_send(q, j):
        r = some(q, j)
        src = latb.at[mine, r]
        send(src, src, up_si, lat_sem(mine, q, j), dev(dz=1), home_up)
        slot = jnp.where(z >= 1, 4, mine)
        send(src, latb.at[slot, r], dn_si, lat_sem(mine, q, j), dev(dz=-1), home_dn)

    def gate(v):
        inner = 0.7978845608028654 * (v + 0.044715 * (v * v * v))
        t = jnp.tanh(inner)
        cdf = 0.5 * (1.0 + t)
        slope = cdf + 0.5 * v * (1.0 - t * t) * (0.7978845608028654 * (1.0 + 0.134145 * (v * v)))
        return v * cdf, slope

    def preact(q, kk):
        v = jnp.dot(xp[q, kk].reshape(128, 2048), we[...], preferred_element_type=F32) + b_ref[...]
        return gate(v)

    def encode(q):
        landed(xp.at[q, k], load_x[q])
        val, slope = preact(q, k)
        val = val.astype(BF)
        own[q] = val
        gp[rows(q, 0), :] = slope

        @pl.when(home)
        def _():
            latb[mine, rows(q, 0), :] = val

    def first_send(q):
        for j in range(SPLIT):
            src = own.at[q, j * SUB : j * SUB + SUB]
            dst, sem = latb.at[mine, some(q, j)], lat_sem(mine, q, SPLIT + j)
            dn_dst = latb.at[jnp.where(z >= 1, 4, mine), some(q, j)]
            send(src, dst, away_up_si, sem, across[0], away_up)
            send(src, dn_dst, away_dn_si, sem, across[1], away_dn)
            send(src, dst, away_si, sem, mate, away)
            origin_send(q, j)

    def send_inputs():
        load_t.wait()
        tg[pl.ds(k * 4 + x, 1)] = t_ref[:, pl.ds(mul(k, 1024), 512)][None]
        for hh in range(2):
            at = 8 + (k * 2 + yh) * 2 + hh
            tg[pl.ds(at, 1)] = t_ref[:, hh * 1024 + 512 : hh * 1024 + 1024][None]
        si = group(tg.at[0:13])
        slot = tg.at[k * 4 + x]
        here, there = pl.ds(mul(k, 1024), 512), pl.ds(mul(1 - k, 1024), 512)
        for d in (1, 2, 3):
            send(t_ref.at[:, here], slot, si, mate_t, dev(dx=d))
            send(t_ref.at[:, there], slot, si, mate_t, across_x[d - 1])
            for hh in range(2):
                at = 8 + (k * 2 + yh) * 2 + hh
                send(t_ref.at[:, hh * 1024 + 512 : hh * 1024 + 1024], tg.at[at], si, mate_t, dev(dy=d))
        send(t_ref.at[:, there], slot, si, mate_t, mate)
        send(xp.at[c, k], xp.at[c, k], group(xp.at[c, k]), mate_x, mate)

    def lat_hop(q, far):
        conds = []
        for m in range(3):
            e = route[m]
            cond = jnp.logical_and(e["on"], jnp.logical_and(e["dist"] == far, e["dist"] < e["reach"]))
            conds.append(cond)
            if not (far == 3 and m == 2):
                sent.append((lat_si[q][m], latb.at[0, 0:256], cond))
        for kk in range(2):
            for m in range(3):
                if far == 3 and m == 2:
                    continue
                e = route[m]

                @pl.when(conds[m])
                def _():
                    for j in range(kk * SPLIT, kk * SPLIT + SPLIT):
                        src = latb.at[jnp.where(e["passing"], 4, m), some(q, j)]
                        dst = latb.at[jnp.where(e["next_passing"], 4, m), some(q, j)]
                        arrived(src, lat_sem(m, q, j))
                        send(src, dst, lat_si[q][m], lat_sem(m, q, j), dev(dz=e["onward"]))

    def lat_last(q):
        for m in range(4):
            e = route[m]

            @pl.when(jnp.logical_and(e["on"], e["dist"] == e["reach"]))
            def _():
                for j in range(2 * SPLIT):
                    arrived(latb.at[m, some(q, j)], lat_sem(m, q, j))

        @pl.when(home)
        def _():
            for j in range(SPLIT, 2 * SPLIT):
                arrived(latb.at[mine, some(q, j)], lat_sem(mine, q, j))

    piece = {}
    for q in range(2):
        for ab in range(2):
            piece[q, ab] = {"core": rnum.take(), "a": rnum.take(), "b": rnum.take(), "g2": rnum.take(3), "g3": rnum.take()}

    def decode(q, ab):
        left = jnp.concatenate([latb[m, q * 256 : q * 256 + 256, :] for m in range(4)], axis=1)
        part = jnp.dot(left, wp[:, ab * 1024 : ab * 1024 + 1024], preferred_element_type=F32)
        p32[q, ab] = part.reshape(2, 2, 64, 1024)
        cs[q, ab] = p32[q, ab, :, o].astype(BF)
        send(cs.at[q, ab], cr.at[q, ab], group(cs.at[q, ab]), piece[q, ab]["core"], dev(flip=1))

    def stage_a(q):
        for ab in range(2):
            arrived(cr.at[q, ab], piece[q, ab]["core"])
            total = (p32[q, ab, :, c] + cr[q, ab].astype(F32)).reshape(4, 2, 16, 1024)
            s32[q, ab] = total
            ys[q, ab] = total.astype(BF)
            wide = ra.at[q] if ab == 0 else rb.at[q]
            si, sem = group(wide), piece[q, ab]["a"]
            for d in (1, 2, 3):
                if ab == 0:
                    to = (y + d) % 4
                    src = ys.at[q, 0, :, to // 2, :, pl.ds(mul(to % 2, 512), 512)]
                    send(src, ra.at[q, d - 1], si, sem, dev(dy=d))
                else:
                    send(ys.at[q, 1, (x + d) % 4], rb.at[q, d - 1], si, sem, dev(dx=d))

    def stage_b(q):
        for ab in range(2):
            buf = ra if ab == 0 else rb
            arrived(buf.at[q], piece[q, ab]["a"])
            if ab == 0:
                total = s32[q, 0, :, yh, :, pl.ds(mul(k, 512), 512)]
            else:
                total = s32[q, 1, x]
            for d in range(3):
                total = total + buf[q, d].astype(F32)
            if ab == 0:
                u32[q, 0] = total
                xs[q, 0] = total.astype(BF)
            else:
                for yy in range(4):
                    block = total[yy // 2, :, (yy % 2) * 512 : (yy % 2) * 512 + 512]
                    u32[q, 1, yy] = block
                    xs[q, 1, yy] = block.astype(BF)
            si, sem = group(rx.at[q, ab]), piece[q, ab]["b"]
            for d in (1, 2, 3):
                to = dev(dx=d) if ab == 0 else dev(dy=d)
                send(xs.at[q, ab], rx.at[q, ab, d - 1], si, sem, to)

    def line_of(q, ab, xx, yy):
        if ab == 0:
            cols = pl.ds(mul(yy % 2, 512), 512)
            return err.at[q, :, c, :, yy // 2, :, cols]
        return err.at[q, xx // 2, c, xx % 2, :, :, 1024:2048]

    def stage_c(q):
        for ab in range(2):
            arrived(rx.at[q, ab], piece[q, ab]["b"])
            total = u32[q, ab]
            for d in range(3):
                total = total + rx[q, ab, d].astype(F32)
            u32[q, ab] = total
            if ab == 0:
                diff = (total - tg[q * 4 : q * 4 + 4].astype(F32)).astype(BF)
                cols = pl.ds(mul(k, 512), 512)
                for xx in range(4):
                    err[q, xx // 2, c, xx % 2, yh, :, cols] = diff[xx]
            else:
                diff = (total - tg[8 + q * 4 : 12 + q * 4].astype(F32)).astype(BF)
                for yy in range(4):
                    start = 1024 + (yy % 2) * 512
                    err[q, x // 2, c, x % 2, yy // 2, :, start : start + 512] = diff[yy]
            line = line_of(q, ab, x, y)
            si = group(ra.at[q])
            for d in (1, 2, 3):
                to = dev(dy=d) if ab == 0 else dev(dx=d)
                send(line, line, si, piece[q, ab]["g2"] + d - 1, to)
            half = err.at[q, :, c, :, :, :, ab * 1024 : ab * 1024 + 1024]
            core_si[q, ab] = group(half)
            send(line, line, core_si[q, ab], piece[q, ab]["g3"], dev(flip=1))
            rc[q, :, ab * 512 : ab * 512 + 512] = u32[q, ab, x if ab == 0 else y].astype(BF)

    core_si = {}

    def stage_e(q):
        for d in (1, 3, 2):
            for ab in range(2):
                line = line_of(q, ab, (x - d + 4) % 4, (y - d + 4) % 4)
                arrived(line, piece[q, ab]["g2"] + d - 1)
                send(line, line, core_si[q, ab], piece[q, ab]["g3"], dev(flip=1))

    def stage_f(q):
        for ab in range(2):
            arrived(err.at[q, :, o, :, :, :, ab * 1024 : ab * 1024 + 1024], piece[q, ab]["g3"])

        for half in range(2):
            out = lax.dot_general(
                err[q].reshape(256, 2048), wp[half * 512 : half * 512 + 512, :],
                (((1,), (1,)), ((), ())), preferred_element_type=F32,
            )
            term[q, 2 * half] = out[:, :256]
            term[q, 2 * half + 1] = out[:, 256:]
            grad_step(q, 0, (2 * half, 2 * half + 1))

    def grad_step(q, depth, members=range(4)):
        for m in members:
            if depth > (3, 3, 2, 0)[m]:
                continue
            e = route[m]
            cond = jnp.logical_and(e["on"], e["reach"] - e["dist"] == depth)
            sent.append((gr_si[q][m], latb.at[0, 0:256], cond))

            @pl.when(cond)
            def _():
                slot = jnp.where(jnp.logical_and(e["dn"], e["dist"] == 1), 4, m)
                for j in range(2 * SPLIT):
                    sem = gr_r + m * (4 * SPLIT) + q * (2 * SPLIT) + j
                    r = slice(q * 256 + j * SUB, q * 256 + j * SUB + SUB)
                    part = term[q, m, j * SUB : j * SUB + SUB, :]
                    if depth:
                        arrived(gr.at[m, r], sem)
                        part = jnp.where(e["passing"], 0.0, part) + gr[m, r, :].astype(F32)
                    gs[m, r, :] = part.astype(BF)
                    sem = gr_r + slot * (4 * SPLIT) + q * (2 * SPLIT) + j
                    send(gs.at[m, r], gr.at[slot, r], gr_si[q][m], sem, dev(dz=e["back"]))

    def finish(q):
        for j in range(2 * SPLIT):
            i = q * 2 * SPLIT + j
            r = slice(i * SUB, i * SUB + SUB)

            @pl.when(home)
            def _():
                lg[...] = term[q, mine, j * SUB : j * SUB + SUB, :]

            @pl.when(home_up)
            def _():
                arrived(gr.at[mine, r], gr_r + mine * (4 * SPLIT) + i)
                lg[...] += gr[mine, r, :].astype(F32)

            @pl.when(home_dn)
            def _():
                arrived(gr.at[4, r], gr_r + 16 * SPLIT + i)
                lg[...] += gr[4, r, :].astype(F32)

            @pl.when(home)
            def _():
                grad = lg[...] * gp[r, :]
                pg[r, :] = grad.astype(BF)
                total = jnp.sum(grad, axis=0, keepdims=True)
                if i == 0:
                    bs[...] = jnp.broadcast_to(total, (8, 256))
                else:
                    bs[...] += jnp.broadcast_to(total, (8, 256))
                send(pg.at[r], pg.at[r], pg_si, pg_r + i, mate)

    def flip_inputs(q, j):
        kk = k if j == 0 else 1 - k
        for i in range(2):
            block = xp[q, kk, :, :, :, :, i * 1024 : i * 1024 + 1024].reshape(128, 1024)
            xt[i * 1024 : i * 1024 + 1024, rows(q, j)] = block.T

    def flip_latents(q):
        for m in range(4):
            lt[m * 256 : m * 256 + 256, q * 256 : q * 256 + 256] = latb[m, q * 256 : q * 256 + 256, :].T

    dec_sem = lnum.take()
    lnum.take()

    def dec_store(i):
        start = pl.multiple_of((i % 2) * 1024 + (i // 2) * 512, 512)
        return pltpu.make_async_copy(dg.at[i % 2], dec_hbm.at[:, pl.ds(start, 512)], ls.at[dec_sem + i % 2])

    def decoder_grads():
        def part(i, _):
            pl.when(i >= 2)(lambda: dec_store(i - 2).wait())
            right = err[:, :, :, :, :, :, pl.ds(mul(i, 512), 512)].reshape(512, 512)
            dg[i % 2] = jnp.dot(lt[...], right, preferred_element_type=F32).astype(BF)
            dec_store(i).start()
            return 0

        lax.fori_loop(0, 4, part, 0)

    load_we.wait()
    load_b.wait()
    encode(0)
    pl.semaphore_wait(barrier, len(peers))
    first_send(0)
    encode(1)
    first_send(1)
    load_w = lnum.take()
    for ab in range(2):
        for hh in range(2):
            local(
                w_hbm.at[:, hh * 1024 + ab * 512 : hh * 1024 + ab * 512 + 512],
                wp.at[:, ab * 1024 + hh * 512 : ab * 1024 + hh * 512 + 512],
                load_w,
            )
    send_inputs()
    clear()
    lat_hop(0, 1)
    lat_hop(1, 1)
    flip_inputs(0, 0)
    lat_hop(0, 2)
    lat_hop(1, 2)
    flip_inputs(1, 0)
    lat_hop(0, 3)
    lat_hop(1, 3)
    lat_last(0)
    landed(wp, load_w)
    decode(0, 0)
    decode(0, 1)
    lat_last(1)
    decode(1, 0)
    stage_a(0)
    decode(1, 1)
    flip_latents(0)
    stage_a(1)
    flip_latents(1)
    arrived(xp.at[c, 1 - k], mate_x)
    send(xp.at[c, 1 - k], xp.at[c, 1 - k], group(xp.at[c, 1 - k]), core_x, dev(flip=1))
    stage_b(0)
    stage_b(1)
    arrived(tg.at[0:13], mate_t)
    arrived(xp.at[o, 1 - k], core_x)
    for q in range(2):
        gp[rows(q, 1), :] = preact(q, 1 - k)[1]
    stage_c(0)
    stage_c(1)
    flip_inputs(0, 1)
    flip_inputs(1, 1)
    xt_copy = local(xt, xt_hbm)
    stage_e(0)
    stage_e(1)
    stage_f(0)
    stage_f(1)
    recs[:, pl.ds(mul(k, 1024), 1024)] = rc[k]
    send(rc.at[1 - k], recs.at[:, pl.ds(mul(k, 1024), 1024)], group(rc.at[1 - k]), mate_rec, mate)
    pl.when(z < 4)(decoder_grads)
    grad_step(0, 1)
    grad_step(1, 1)
    grad_step(0, 2)
    grad_step(1, 2)
    grad_step(0, 3)
    grad_step(1, 3)
    pl.when(z >= 4)(decoder_grads)
    finish(0)
    finish(1)
    send(bs, bs, group(bs, home), mate_bias, mate, home)
    for i in range(4 * SPLIT):
        arrived(pg.at[i * SUB : i * SUB + SUB], pg_r + i, away)

    pg_copy = local(pg, pg_hbm)
    arrived(bs, mate_bias, away)
    bias_copy = local(bs.at[0:1], bias_hbm)
    arrived(recs.at[:, pl.ds(mul(1 - k, 1024), 1024)], mate_rec)
    rec_copy = local(recs, rec_hbm)
    for si, like, cond in sent:
        copy = rc_(like, like, si, 0, mate)
        if cond is None:
            copy.wait_send()
        else:
            pl.when(cond)(copy.wait_send)
    dec_store(2).wait()
    dec_store(3).wait()
    for copy in (xt_copy, pg_copy, bias_copy, rec_copy):
        copy.wait()
    assert (snum.count, rnum.count, lnum.count) == COUNTS, (snum.count, rnum.count, lnum.count)


def outputs(rec_in, bias_in, pg_hbm, xt_hbm, dec_in, rec, enc, bias, dec, recv, biasv, pg, xt, encv, decv, sem):
    def part(i):
        return pl.ds(i * 256, 256)

    loads = [pltpu.make_async_copy(pg_hbm, pg, sem.at[0]), pltpu.make_async_copy(xt_hbm, xt, sem.at[1])]
    dec_loads = [pltpu.make_async_copy(dec_in.at[part(i)], decv.at[part(i)], sem.at[2 + i]) for i in range(4)]
    dec_stores = [pltpu.make_async_copy(decv.at[part(i)], dec.at[part(i)], sem.at[6 + i]) for i in range(4)]
    enc_store = pltpu.make_async_copy(encv, enc, sem.at[10])
    small_loads = [pltpu.make_async_copy(rec_in, recv, sem.at[11]), pltpu.make_async_copy(bias_in, biasv, sem.at[12])]
    small_stores = [pltpu.make_async_copy(recv, rec, sem.at[13]), pltpu.make_async_copy(biasv, bias, sem.at[14])]
    for copy in loads + dec_loads + small_loads:
        copy.start()
    for copy in loads:
        copy.wait()
    for i in range(2):
        dec_loads[i].wait()
        dec_stores[i].start()
    encv[...] = jnp.dot(xt[...], pg[...], preferred_element_type=F32).astype(BF)
    enc_store.start()
    for i in range(2, 4):
        dec_loads[i].wait()
        dec_stores[i].start()
    for load, store in zip(small_loads, small_stores):
        load.wait()
        store.start()
    for copy in dec_stores + small_stores + [enc_store]:
        copy.wait()


def kernel1(layer_inputs, layer_targets, encoder_weight, encoder_bias, decoder_weight):
    vm, hbm = pl.BlockSpec(memory_space=pltpu.VMEM), pl.BlockSpec(memory_space=pl.ANY)
    scratch = [
        pltpu.VMEM((16, 2048), BF),
        pltpu.VMEM((1, 256), F32),
        pltpu.VMEM((2, 2, 2, 2, 2, 16, 2048), BF),
        pltpu.VMEM((2048, 512), BF),
        pltpu.VMEM((2048, 256), BF),
        pltpu.VMEM((1024, 2048), BF),
        pltpu.VMEM((2, 128, 256), BF),
        pltpu.VMEM((5, 512, 256), BF),
        pltpu.VMEM((1024, 512), BF),
        pltpu.VMEM((512, 256), F32),
        pltpu.VMEM((16, 16, 512), BF),
        pltpu.VMEM((2, 2, 2, 2, 64, 1024), F32),
        pltpu.VMEM((2, 2, 2, 64, 1024), BF),
        pltpu.VMEM((2, 2, 2, 64, 1024), BF),
        pltpu.VMEM((2, 2, 4, 2, 16, 1024), F32),
        pltpu.VMEM((2, 2, 4, 2, 16, 1024), BF),
        pltpu.VMEM((2, 3, 4, 16, 512), BF),
        pltpu.VMEM((2, 3, 2, 16, 1024), BF),
        pltpu.VMEM((2, 2, 4, 16, 512), F32),
        pltpu.VMEM((2, 2, 4, 16, 512), BF),
        pltpu.VMEM((2, 2, 3, 4, 16, 512), BF),
        pltpu.VMEM((2, 16, 1024), BF),
        pltpu.VMEM((2, 2, 2, 2, 2, 16, 2048), BF),
        pltpu.VMEM((2, 4, 256, 256), F32),
        pltpu.VMEM((5, 512, 256), BF),
        pltpu.VMEM((4, 512, 256), BF),
        pltpu.VMEM((SUB, 256), F32),
        pltpu.VMEM((512, 256), BF),
        pltpu.VMEM((8, 256), F32),
        pltpu.VMEM((16, 2048), BF),
        pltpu.VMEM((2, 1024, 512), BF),
        *[pltpu.SemaphoreType.DMA((n,)) for n in COUNTS],
    ]
    rec, bias, pg, xt, dec = pl.pallas_call(
        kernel,
        out_shape=(
            jax.ShapeDtypeStruct((16, 2048), BF),
            jax.ShapeDtypeStruct((1, 256), F32),
            jax.ShapeDtypeStruct((512, 256), BF),
            jax.ShapeDtypeStruct((2048, 512), BF),
            jax.ShapeDtypeStruct((1024, 2048), BF),
        ),
        in_specs=[hbm] * 5,
        out_specs=[hbm] * 5,
        scratch_shapes=scratch,
        compiler_params=pltpu.CompilerParams(
            collective_id=0, has_side_effects=True, vmem_limit_bytes=56 * 1024 * 1024
        ),
        name="transcoder_step",
    )(
        layer_inputs.reshape(2, 2, 2, 2, 16, 2048),
        layer_targets[0],
        encoder_weight[0],
        encoder_bias,
        decoder_weight.reshape(1024, 2048),
    )
    return rec, bias, pg, xt, dec


def shards(*args):
    vm, hbm = pl.BlockSpec(memory_space=pltpu.VMEM), pl.BlockSpec(memory_space=pl.ANY)
    rec, bias, pg, xt, dec = kernel1(*args)
    rec, enc, bias, dec = pl.pallas_call(
        outputs,
        out_shape=(
            jax.ShapeDtypeStruct((16, 2048), BF),
            jax.ShapeDtypeStruct((2048, 256), BF),
            jax.ShapeDtypeStruct((1, 256), F32),
            jax.ShapeDtypeStruct((1024, 2048), BF),
        ),
        in_specs=[hbm] * 5,
        out_specs=[hbm] * 4,
        scratch_shapes=[
            pltpu.VMEM((16, 2048), BF),
            pltpu.VMEM((1, 256), F32),
            pltpu.VMEM((512, 256), BF),
            pltpu.VMEM((2048, 512), BF),
            pltpu.VMEM((2048, 256), BF),
            pltpu.VMEM((1024, 2048), BF),
            pltpu.SemaphoreType.DMA((15,)),
        ],
        compiler_params=pltpu.CompilerParams(vmem_limit_bytes=56 * 1024 * 1024),
        name="write_outputs",
    )(rec, bias, pg, xt, dec)
    return rec[None], enc[None], bias, dec.reshape(1, 4, 1, 256, 2048)


def solution(mesh):
    placed = (
        P("layer", "tok", None),
        P("layer", ("latent", "tok"), None),
        P("layer", None, "latent"),
        P("layer", "latent"),
        P("layer", None, "tok", "latent", None),
    )
    return jax.shard_map(
        shards,
        mesh=mesh,
        in_specs=placed,
        out_specs=(
            P("layer", ("latent", "tok"), None),
            P("layer", None, "latent"),
            P("layer", "latent"),
            P("layer", None, "tok", "latent", None),
        ),
        check_vma=False,
    )
```

```python
import jax
import jax.numpy as jnp
from jax import lax
from jax.experimental import pallas as pl
from jax.experimental.pallas import tpu as pltpu
from jax.sharding import PartitionSpec as P

MESH = pl.DeviceIdType.MESH
SPLIT = 2
SUB = 128 // SPLIT
COUNTS = (45, 113, 6)
BF = jnp.bfloat16
F32 = jnp.float32


def mul(value, by):
    return pl.multiple_of(value * by, by)


class Numbers:
    def __init__(self):
        self.count = 0

    def take(self, n=1):
        base = self.count
        self.count += n
        return base


def kernel(
    x_hbm, t_hbm, we_hbm, b_hbm, w_hbm,
    rec_out, bias_out, pg_out, xt, dec_out,
    t_ref, b_ref, xp, we, wp, own, latb, lt, gp, tg, p32, cs, cr, s32, ys, ra, rb, u32, xs, rx, rc, err,
    term, gr, gs, lg, pg, bs, recs, ss, rs, ls,
):
    z, lat, k = lax.axis_index("layer"), lax.axis_index("latent"), lax.axis_index("tok")
    x, yh, c = lat // 4, (lat // 2) % 2, lat % 2
    y = yh * 2 + k
    h = z % 2
    o = 1 - c

    def dev(dx=0, dy=0, dz=0, flip=0):
        xx, yy, zz = (x + dx) % 4, (y + dy) % 4, (z + dz) % 8
        cc = o if flip else c
        return (zz, xx * 4 + (yy // 2) * 2 + cc, yy % 2)

    mate = (z, lat, 1 - k)
    snum, rnum, lnum = Numbers(), Numbers(), Numbers()
    sent = []

    def rc_(src, dst, si, ri, to):
        return pltpu.make_async_remote_copy(
            src_ref=src, dst_ref=dst, send_sem=ss.at[si], recv_sem=rs.at[ri],
            device_id=to, device_id_type=MESH,
        )

    def group(like, cond=None):
        si = snum.take()
        sent.append((si, like, cond))
        return si

    def send(src, dst, si, ri, to, cond=None):
        copy = rc_(src, dst, si, ri, to)
        if cond is None:
            copy.start()
        else:
            pl.when(cond)(copy.start)

    def arrived(dst, ri, cond=None):
        copy = rc_(dst, dst, 0, ri, mate)
        if cond is None:
            copy.wait_recv()
        else:
            pl.when(cond)(copy.wait_recv)

    def local(src, dst, li=None):
        copy = pltpu.make_async_copy(src, dst, ls.at[lnum.take() if li is None else li])
        copy.start()
        return copy

    def landed(dst, li):
        pltpu.make_async_copy(dst, dst, ls.at[li]).wait()

    load_x = [lnum.take(), lnum.take()]
    for cc in range(2):
        local(x_hbm.at[:, :, cc, 0], xp.at[0, k, cc], load_x[0])
    load_we = local(we_hbm, we)
    load_b = local(b_hbm, b_ref)
    for cc in range(2):
        local(x_hbm.at[:, :, cc, 1], xp.at[1, k, cc], load_x[1])

    load_t = local(t_hbm, t_ref)

    barrier = pltpu.get_barrier_semaphore()
    peers = [dev(dz=1), dev(dz=-1), dev(flip=1)]
    peers += [dev(dy=d) for d in (1, 2, 3)] + [dev(dx=d) for d in (1, 2, 3)]
    across = [((z + 1) % 8, lat, 1 - k), ((z + 7) % 8, lat, 1 - k)]
    across_x = [(z, (x + d) % 4 * 4 + yh * 2 + c, 1 - k) for d in (1, 2, 3)]
    peers += across + across_x
    for to in peers:
        pl.semaphore_signal(barrier, inc=1, device_id=to, device_id_type=MESH)

    ku = [4, 4, 3 - k, 1 - k]
    kd = [3, 3 * (1 - k), 0, 0]
    route = []
    for m in range(4):
        s = 2 * m + k
        u, d = z - s, (s - z + 8) % 8
        on_up = jnp.logical_and(u >= 1, u <= ku[m])
        on_dn = jnp.logical_and(d >= 1, d <= kd[m])
        on = jnp.logical_or(on_up, on_dn)
        dist = jnp.where(on_up, u, d)
        reach = jnp.where(on_up, ku[m], kd[m])
        passing = jnp.logical_and(on_dn, z < s)
        next_passing = jnp.logical_and(on_dn, (z + 7) % 8 < s)
        next_passing = jnp.logical_and(next_passing, z > 0)
        route.append(dict(on=on, up=on_up, dn=on_dn, dist=dist, reach=reach, passing=passing,
                          next_passing=next_passing, valid=s <= z,
                          onward=jnp.where(on_up, 1, 7), back=jnp.where(on_up, 7, 1)))
    mine = z // 2
    home = k == h
    ku_own = jnp.where(mine == 0, 4, jnp.where(mine == 1, 4, jnp.where(mine == 2, 3 - h, 1 - h)))
    kd_own = jnp.where(mine == 0, 3, jnp.where(mine == 1, 3 * (1 - h), 0))
    home_up = jnp.logical_and(home, ku_own > 0)
    home_dn = jnp.logical_and(home, kd_own > 0)
    away = jnp.logical_not(home)
    away_up = jnp.logical_and(away, ku_own > 0)
    away_dn = jnp.logical_and(away, kd_own > 0)

    def clear():
        for m in range(4):
            @pl.when(jnp.logical_not(route[m]["valid"]))
            def _():
                latb[m] = jnp.zeros((512, 256), BF)

    lat_r = rnum.take(16 * SPLIT)
    mate_x, core_x, mate_t, mate_rec, mate_bias = (rnum.take() for _ in range(5))
    pg_r = rnum.take(4 * SPLIT)
    gr_r = rnum.take(20 * SPLIT)

    def lat_sem(m, q, j):
        return lat_r + m * (4 * SPLIT) + q * (2 * SPLIT) + j

    def rows(q, j):
        kk = k if j == 0 else 1 - k
        return pl.ds(pl.multiple_of(q * 256 + kk * 128, 128), 128)

    def some(q, j):
        kk = k if j < SPLIT else 1 - k
        return pl.ds(pl.multiple_of(q * 256 + kk * 128 + (j % SPLIT) * SUB, SUB), SUB)

    up_si, dn_si = group(own, home_up), group(own, home_dn)
    away_si, pg_si = group(own, away), group(pg, home)
    away_up_si, away_dn_si = group(own, away_up), group(own, away_dn)
    lat_si = [[snum.take() for m in range(3)] for q in range(2)]
    gr_si = [[snum.take() for m in range(4)] for q in range(2)]

    def origin_send(q, j):
        r = some(q, j)
        src = latb.at[mine, r]
        send(src, src, up_si, lat_sem(mine, q, j), dev(dz=1), home_up)
        slot = jnp.where(z >= 1, 4, mine)
        send(src, latb.at[slot, r], dn_si, lat_sem(mine, q, j), dev(dz=-1), home_dn)

    def gate(v):
        inner = 0.7978845608028654 * (v + 0.044715 * (v * v * v))
        t = jnp.tanh(inner)
        cdf = 0.5 * (1.0 + t)
        slope = cdf + 0.5 * v * (1.0 - t * t) * (0.7978845608028654 * (1.0 + 0.134145 * (v * v)))
        return v * cdf, slope

    def preact(q, kk):
        v = jnp.dot(xp[q, kk].reshape(128, 2048), we[...], preferred_element_type=F32) + b_ref[...]
        return gate(v)

    def encode(q):
        landed(xp.at[q, k], load_x[q])
        val, slope = preact(q, k)
        val = val.astype(BF)
        own[q] = val
        gp[rows(q, 0), :] = slope

        @pl.when(home)
        def _():
            latb[mine, rows(q, 0), :] = val

    def first_send(q):
        for j in range(SPLIT):
            src = own.at[q, j * SUB : j * SUB + SUB]
            dst, sem = latb.at[mine, some(q, j)], lat_sem(mine, q, SPLIT + j)
            dn_dst = latb.at[jnp.where(z >= 1, 4, mine), some(q, j)]
            send(src, dst, away_up_si, sem, across[0], away_up)
            send(src, dn_dst, away_dn_si, sem, across[1], away_dn)
            send(src, dst, away_si, sem, mate, away)
            origin_send(q, j)

    def send_inputs():
        load_t.wait()
        tg[pl.ds(k * 4 + x, 1)] = t_ref[:, pl.ds(mul(k, 1024), 512)][None]
        for hh in range(2):
            at = 8 + (k * 2 + yh) * 2 + hh
            tg[pl.ds(at, 1)] = t_ref[:, hh * 1024 + 512 : hh * 1024 + 1024][None]
        si = group(tg.at[0:13])
        slot = tg.at[k * 4 + x]
        here, there = pl.ds(mul(k, 1024), 512), pl.ds(mul(1 - k, 1024), 512)
        for d in (1, 2, 3):
            send(t_ref.at[:, here], slot, si, mate_t, dev(dx=d))
            send(t_ref.at[:, there], slot, si, mate_t, across_x[d - 1])
            for hh in range(2):
                at = 8 + (k * 2 + yh) * 2 + hh
                send(t_ref.at[:, hh * 1024 + 512 : hh * 1024 + 1024], tg.at[at], si, mate_t, dev(dy=d))
        send(t_ref.at[:, there], slot, si, mate_t, mate)
        send(xp.at[c, k], xp.at[c, k], group(xp.at[c, k]), mate_x, mate)

    def lat_hop(q, far):
        conds = []
        for m in range(3):
            e = route[m]
            cond = jnp.logical_and(e["on"], jnp.logical_and(e["dist"] == far, e["dist"] < e["reach"]))
            conds.append(cond)
            if not (far == 3 and m == 2):
                sent.append((lat_si[q][m], latb.at[0, 0:256], cond))
        for kk in range(2):
            for m in range(3):
                if far == 3 and m == 2:
                    continue
                e = route[m]

                @pl.when(conds[m])
                def _():
                    for j in range(kk * SPLIT, kk * SPLIT + SPLIT):
                        src = latb.at[jnp.where(e["passing"], 4, m), some(q, j)]
                        dst = latb.at[jnp.where(e["next_passing"], 4, m), some(q, j)]
                        arrived(src, lat_sem(m, q, j))
                        send(src, dst, lat_si[q][m], lat_sem(m, q, j), dev(dz=e["onward"]))

    def lat_last(q):
        for m in range(4):
            e = route[m]

            @pl.when(jnp.logical_and(e["on"], e["dist"] == e["reach"]))
            def _():
                for j in range(2 * SPLIT):
                    arrived(latb.at[m, some(q, j)], lat_sem(m, q, j))

        @pl.when(home)
        def _():
            for j in range(SPLIT, 2 * SPLIT):
                arrived(latb.at[mine, some(q, j)], lat_sem(mine, q, j))

    piece = {}
    for q in range(2):
        for ab in range(2):
            piece[q, ab] = {"core": rnum.take(), "a": rnum.take(), "b": rnum.take(), "g2": rnum.take(3), "g3": rnum.take()}

    def decode(q, ab):
        left = jnp.concatenate([latb[m, q * 256 : q * 256 + 256, :] for m in range(4)], axis=1)
        part = jnp.dot(left, wp[:, ab * 1024 : ab * 1024 + 1024], preferred_element_type=F32)
        p32[q, ab] = part.reshape(2, 2, 64, 1024)
        cs[q, ab] = p32[q, ab, :, o].astype(BF)
        send(cs.at[q, ab], cr.at[q, ab], group(cs.at[q, ab]), piece[q, ab]["core"], dev(flip=1))

    def stage_a(q):
        for ab in range(2):
            arrived(cr.at[q, ab], piece[q, ab]["core"])
            total = (p32[q, ab, :, c] + cr[q, ab].astype(F32)).reshape(4, 2, 16, 1024)
            s32[q, ab] = total
            ys[q, ab] = total.astype(BF)
            wide = ra.at[q] if ab == 0 else rb.at[q]
            si, sem = group(wide), piece[q, ab]["a"]
            for d in (1, 2, 3):
                if ab == 0:
                    to = (y + d) % 4
                    src = ys.at[q, 0, :, to // 2, :, pl.ds(mul(to % 2, 512), 512)]
                    send(src, ra.at[q, d - 1], si, sem, dev(dy=d))
                else:
                    send(ys.at[q, 1, (x + d) % 4], rb.at[q, d - 1], si, sem, dev(dx=d))

    def stage_b(q):
        for ab in range(2):
            buf = ra if ab == 0 else rb
            arrived(buf.at[q], piece[q, ab]["a"])
            if ab == 0:
                total = s32[q, 0, :, yh, :, pl.ds(mul(k, 512), 512)]
            else:
                total = s32[q, 1, x]
            for d in range(3):
                total = total + buf[q, d].astype(F32)
            if ab == 0:
                u32[q, 0] = total
                xs[q, 0] = total.astype(BF)
            else:
                for yy in range(4):
                    block = total[yy // 2, :, (yy % 2) * 512 : (yy % 2) * 512 + 512]
                    u32[q, 1, yy] = block
                    xs[q, 1, yy] = block.astype(BF)
            si, sem = group(rx.at[q, ab]), piece[q, ab]["b"]
            for d in (1, 2, 3):
                to = dev(dx=d) if ab == 0 else dev(dy=d)
                send(xs.at[q, ab], rx.at[q, ab, d - 1], si, sem, to)

    def line_of(q, ab, xx, yy):
        if ab == 0:
            cols = pl.ds(mul(yy % 2, 512), 512)
            return err.at[q, :, c, :, yy // 2, :, cols]
        return err.at[q, xx // 2, c, xx % 2, :, :, 1024:2048]

    def stage_c(q):
        for ab in range(2):
            arrived(rx.at[q, ab], piece[q, ab]["b"])
            total = u32[q, ab]
            for d in range(3):
                total = total + rx[q, ab, d].astype(F32)
            u32[q, ab] = total
            if ab == 0:
                diff = (total - tg[q * 4 : q * 4 + 4].astype(F32)).astype(BF)
                cols = pl.ds(mul(k, 512), 512)
                for xx in range(4):
                    err[q, xx // 2, c, xx % 2, yh, :, cols] = diff[xx]
            else:
                diff = (total - tg[8 + q * 4 : 12 + q * 4].astype(F32)).astype(BF)
                for yy in range(4):
                    start = 1024 + (yy % 2) * 512
                    err[q, x // 2, c, x % 2, yy // 2, :, start : start + 512] = diff[yy]
            line = line_of(q, ab, x, y)
            si = group(ra.at[q])
            for d in (1, 2, 3):
                to = dev(dy=d) if ab == 0 else dev(dx=d)
                send(line, line, si, piece[q, ab]["g2"] + d - 1, to)
            half = err.at[q, :, c, :, :, :, ab * 1024 : ab * 1024 + 1024]
            core_si[q, ab] = group(half)
            send(line, line, core_si[q, ab], piece[q, ab]["g3"], dev(flip=1))
            rc[q, :, ab * 512 : ab * 512 + 512] = u32[q, ab, x if ab == 0 else y].astype(BF)

    core_si = {}

    def stage_e(q):
        for d in (1, 3, 2):
            for ab in range(2):
                line = line_of(q, ab, (x - d + 4) % 4, (y - d + 4) % 4)
                arrived(line, piece[q, ab]["g2"] + d - 1)
                send(line, line, core_si[q, ab], piece[q, ab]["g3"], dev(flip=1))

    def stage_f(q):
        for ab in range(2):
            arrived(err.at[q, :, o, :, :, :, ab * 1024 : ab * 1024 + 1024], piece[q, ab]["g3"])

        for half in range(2):
            out = lax.dot_general(
                err[q].reshape(256, 2048), wp[half * 512 : half * 512 + 512, :],
                (((1,), (1,)), ((), ())), preferred_element_type=F32,
            )
            term[q, 2 * half] = out[:, :256]
            term[q, 2 * half + 1] = out[:, 256:]
            grad_step(q, 0, (2 * half, 2 * half + 1))

    def grad_step(q, depth, members=range(4)):
        for m in members:
            if depth > (3, 3, 2, 0)[m]:
                continue
            e = route[m]
            cond = jnp.logical_and(e["on"], e["reach"] - e["dist"] == depth)
            sent.append((gr_si[q][m], latb.at[0, 0:256], cond))

            @pl.when(cond)
            def _():
                slot = jnp.where(jnp.logical_and(e["dn"], e["dist"] == 1), 4, m)
                for j in range(2 * SPLIT):
                    sem = gr_r + m * (4 * SPLIT) + q * (2 * SPLIT) + j
                    r = slice(q * 256 + j * SUB, q * 256 + j * SUB + SUB)
                    part = term[q, m, j * SUB : j * SUB + SUB, :]
                    if depth:
                        arrived(gr.at[m, r], sem)
                        part = jnp.where(e["passing"], 0.0, part) + gr[m, r, :].astype(F32)
                    gs[m, r, :] = part.astype(BF)
                    sem = gr_r + slot * (4 * SPLIT) + q * (2 * SPLIT) + j
                    send(gs.at[m, r], gr.at[slot, r], gr_si[q][m], sem, dev(dz=e["back"]))

    def finish(q):
        for j in range(2 * SPLIT):
            i = q * 2 * SPLIT + j
            r = slice(i * SUB, i * SUB + SUB)

            @pl.when(home)
            def _():
                lg[...] = term[q, mine, j * SUB : j * SUB + SUB, :]

            @pl.when(home_up)
            def _():
                arrived(gr.at[mine, r], gr_r + mine * (4 * SPLIT) + i)
                lg[...] += gr[mine, r, :].astype(F32)

            @pl.when(home_dn)
            def _():
                arrived(gr.at[4, r], gr_r + 16 * SPLIT + i)
                lg[...] += gr[4, r, :].astype(F32)

            @pl.when(home)
            def _():
                grad = lg[...] * gp[r, :]
                pg[r, :] = grad.astype(BF)
                total = jnp.sum(grad, axis=0, keepdims=True)
                if i == 0:
                    bs[...] = jnp.broadcast_to(total, (8, 256))
                else:
                    bs[...] += jnp.broadcast_to(total, (8, 256))
                send(pg.at[r], pg.at[r], pg_si, pg_r + i, mate)

    def flip_inputs(q, j):
        kk = k if j == 0 else 1 - k
        for i in range(2):
            block = xp[q, kk, :, :, :, :, i * 1024 : i * 1024 + 1024].reshape(128, 1024)
            xt[i * 1024 : i * 1024 + 1024, rows(q, j)] = block.T

    def flip_latents(q):
        for m in range(4):
            lt[m * 256 : m * 256 + 256, q * 256 : q * 256 + 256] = latb[m, q * 256 : q * 256 + 256, :].T

    def decoder_grads():
        def part(i, _):
            right = err[:, :, :, :, :, :, pl.ds(mul(i, 512), 512)].reshape(512, 512)
            start = pl.multiple_of((i % 2) * 1024 + (i // 2) * 512, 512)
            dec_out[:, pl.ds(start, 512)] = jnp.dot(lt[...], right, preferred_element_type=F32).astype(BF)
            return 0

        lax.fori_loop(0, 4, part, 0)

    load_we.wait()
    load_b.wait()
    encode(0)
    pl.semaphore_wait(barrier, len(peers))
    first_send(0)
    encode(1)
    first_send(1)
    load_w = lnum.take()
    for ab in range(2):
        for hh in range(2):
            local(
                w_hbm.at[:, hh * 1024 + ab * 512 : hh * 1024 + ab * 512 + 512],
                wp.at[:, ab * 1024 + hh * 512 : ab * 1024 + hh * 512 + 512],
                load_w,
            )
    send_inputs()
    clear()
    lat_hop(0, 1)
    lat_hop(1, 1)
    flip_inputs(0, 0)
    lat_hop(0, 2)
    lat_hop(1, 2)
    flip_inputs(1, 0)
    lat_hop(0, 3)
    lat_hop(1, 3)
    lat_last(0)
    landed(wp, load_w)
    decode(0, 0)
    decode(0, 1)
    lat_last(1)
    decode(1, 0)
    stage_a(0)
    decode(1, 1)
    flip_latents(0)
    stage_a(1)
    flip_latents(1)
    arrived(xp.at[c, 1 - k], mate_x)
    send(xp.at[c, 1 - k], xp.at[c, 1 - k], group(xp.at[c, 1 - k]), core_x, dev(flip=1))
    stage_b(0)
    stage_b(1)
    arrived(tg.at[0:13], mate_t)
    arrived(xp.at[o, 1 - k], core_x)
    for q in range(2):
        gp[rows(q, 1), :] = preact(q, 1 - k)[1]
    stage_c(0)
    stage_c(1)
    flip_inputs(0, 1)
    flip_inputs(1, 1)
    stage_e(0)
    stage_e(1)
    stage_f(0)
    stage_f(1)
    recs[:, pl.ds(mul(k, 1024), 1024)] = rc[k]
    send(rc.at[1 - k], recs.at[:, pl.ds(mul(k, 1024), 1024)], group(rc.at[1 - k]), mate_rec, mate)
    pl.when(z < 4)(decoder_grads)
    grad_step(0, 1)
    grad_step(1, 1)
    grad_step(0, 2)
    grad_step(1, 2)
    grad_step(0, 3)
    grad_step(1, 3)
    pl.when(z >= 4)(decoder_grads)
    finish(0)
    finish(1)
    send(bs, bs, group(bs, home), mate_bias, mate, home)
    for i in range(4 * SPLIT):
        arrived(pg.at[i * SUB : i * SUB + SUB], pg_r + i, away)

    pg_out[...] = pg[...]
    arrived(bs, mate_bias, away)
    bias_out[...] = bs[0:1, :]
    arrived(recs.at[:, pl.ds(mul(1 - k, 1024), 1024)], mate_rec)
    rec_out[...] = recs[...]
    for si, like, cond in sent:
        copy = rc_(like, like, si, 0, mate)
        if cond is None:
            copy.wait_send()
        else:
            pl.when(cond)(copy.wait_send)
    assert (snum.count, rnum.count, lnum.count) == COUNTS, (snum.count, rnum.count, lnum.count)


def outputs(rec_in, bias_in, pg, xt, dec_in, rec, enc, bias, dec, encv, sem):
    copies = [
        pltpu.make_async_copy(dec_in, dec, sem.at[0]),
        pltpu.make_async_copy(rec_in, rec, sem.at[1]),
        pltpu.make_async_copy(bias_in, bias, sem.at[2]),
        pltpu.make_async_copy(encv, enc, sem.at[3]),
    ]
    for copy in copies[:3]:
        copy.start()
    encv[...] = jnp.dot(xt[...], pg[...], preferred_element_type=F32).astype(BF)
    copies[3].start()
    for copy in copies:
        copy.wait()


def kernel1(layer_inputs, layer_targets, encoder_weight, encoder_bias, decoder_weight):
    vm, hbm = pl.BlockSpec(memory_space=pltpu.VMEM), pl.BlockSpec(memory_space=pl.ANY)
    scratch = [
        pltpu.VMEM((16, 2048), BF),
        pltpu.VMEM((1, 256), F32),
        pltpu.VMEM((2, 2, 2, 2, 2, 16, 2048), BF),
        pltpu.VMEM((2048, 256), BF),
        pltpu.VMEM((1024, 2048), BF),
        pltpu.VMEM((2, 128, 256), BF),
        pltpu.VMEM((5, 512, 256), BF),
        pltpu.VMEM((1024, 512), BF),
        pltpu.VMEM((512, 256), F32),
        pltpu.VMEM((16, 16, 512), BF),
        pltpu.VMEM((2, 2, 2, 2, 64, 1024), F32),
        pltpu.VMEM((2, 2, 2, 64, 1024), BF),
        pltpu.VMEM((2, 2, 2, 64, 1024), BF),
        pltpu.VMEM((2, 2, 4, 2, 16, 1024), F32),
        pltpu.VMEM((2, 2, 4, 2, 16, 1024), BF),
        pltpu.VMEM((2, 3, 4, 16, 512), BF),
        pltpu.VMEM((2, 3, 2, 16, 1024), BF),
        pltpu.VMEM((2, 2, 4, 16, 512), F32),
        pltpu.VMEM((2, 2, 4, 16, 512), BF),
        pltpu.VMEM((2, 2, 3, 4, 16, 512), BF),
        pltpu.VMEM((2, 16, 1024), BF),
        pltpu.VMEM((2, 2, 2, 2, 2, 16, 2048), BF),
        pltpu.VMEM((2, 4, 256, 256), F32),
        pltpu.VMEM((5, 512, 256), BF),
        pltpu.VMEM((4, 512, 256), BF),
        pltpu.VMEM((SUB, 256), F32),
        pltpu.VMEM((512, 256), BF),
        pltpu.VMEM((8, 256), F32),
        pltpu.VMEM((16, 2048), BF),
        *[pltpu.SemaphoreType.DMA((n,)) for n in COUNTS],
    ]
    rec, bias, pg, xt, dec = pl.pallas_call(
        kernel,
        out_shape=(
            pltpu.VMEM((16, 2048), BF),
            pltpu.VMEM((1, 256), F32),
            pltpu.VMEM((512, 256), BF),
            pltpu.VMEM((2048, 512), BF),
            pltpu.VMEM((1024, 2048), BF),
        ),
        in_specs=[hbm] * 5,
        out_specs=[vm] * 5,
        scratch_shapes=scratch,
        compiler_params=pltpu.CompilerParams(
            collective_id=0, has_side_effects=True, vmem_limit_bytes=48 * 1024 * 1024
        ),
        name="transcoder_step",
    )(
        layer_inputs.reshape(2, 2, 2, 2, 16, 2048),
        layer_targets[0],
        encoder_weight[0],
        encoder_bias,
        decoder_weight.reshape(1024, 2048),
    )
    return rec, bias, pg, xt, dec


def shards(*args):
    vm, hbm = pl.BlockSpec(memory_space=pltpu.VMEM), pl.BlockSpec(memory_space=pl.ANY)
    rec, bias, pg, xt, dec = kernel1(*args)
    rec, enc, bias, dec = pl.pallas_call(
        outputs,
        out_shape=(
            jax.ShapeDtypeStruct((16, 2048), BF),
            jax.ShapeDtypeStruct((2048, 256), BF),
            jax.ShapeDtypeStruct((1, 256), F32),
            jax.ShapeDtypeStruct((1024, 2048), BF),
        ),
        in_specs=[vm] * 5,
        out_specs=[hbm] * 4,
        scratch_shapes=[pltpu.VMEM((2048, 256), BF), pltpu.SemaphoreType.DMA((4,))],
        compiler_params=pltpu.CompilerParams(vmem_limit_bytes=16 * 1024 * 1024),
        name="write_outputs",
    )(rec, bias, pg, xt, dec)
    return rec[None], enc[None], bias, dec.reshape(1, 4, 1, 256, 2048)


def solution(mesh):
    placed = (
        P("layer", "tok", None),
        P("layer", ("latent", "tok"), None),
        P("layer", None, "latent"),
        P("layer", "latent"),
        P("layer", None, "tok", "latent", None),
    )
    return jax.shard_map(
        shards,
        mesh=mesh,
        in_specs=placed,
        out_specs=(
            P("layer", ("latent", "tok"), None),
            P("layer", None, "latent"),
            P("layer", "latent"),
            P("layer", None, "tok", "latent", None),
        ),
        check_vma=False,
    )
```

```python
import jax
import jax.numpy as jnp
from jax import lax
from jax.experimental import pallas as pl
from jax.experimental.pallas import tpu as pltpu
from jax.sharding import PartitionSpec as P

MESH = pl.DeviceIdType.MESH
SPLIT = 2
SUB = 128 // SPLIT
COUNTS = (46, 114, 6)
BF = jnp.bfloat16
F32 = jnp.float32


def mul(value, by):
    return pl.multiple_of(value * by, by)


class Numbers:
    def __init__(self):
        self.count = 0

    def take(self, n=1):
        base = self.count
        self.count += n
        return base


def kernel(
    x_hbm, t_hbm, we_hbm, b_hbm, w_hbm,
    rec_out, bias_out, pg_out, xt, dec_out,
    t_ref, b_ref, xp, we, wp, own, latb, lt, gp, tg, p32, cs, cr, s32, ys, ra, rb, u32, xs, rx, rc, err,
    term, gr, gs, lg, pg, bs, recs, ss, rs, ls,
):
    z, lat, k = lax.axis_index("layer"), lax.axis_index("latent"), lax.axis_index("tok")
    x, yh, c = lat // 4, (lat // 2) % 2, lat % 2
    y = yh * 2 + k
    h = z % 2
    o = 1 - c

    def dev(dx=0, dy=0, dz=0, flip=0):
        xx, yy, zz = (x + dx) % 4, (y + dy) % 4, (z + dz) % 8
        cc = o if flip else c
        return (zz, xx * 4 + (yy // 2) * 2 + cc, yy % 2)

    mate = (z, lat, 1 - k)
    snum, rnum, lnum = Numbers(), Numbers(), Numbers()
    sent = []

    def rc_(src, dst, si, ri, to):
        return pltpu.make_async_remote_copy(
            src_ref=src, dst_ref=dst, send_sem=ss.at[si], recv_sem=rs.at[ri],
            device_id=to, device_id_type=MESH,
        )

    def group(like, cond=None):
        si = snum.take()
        sent.append((si, like, cond))
        return si

    def send(src, dst, si, ri, to, cond=None):
        copy = rc_(src, dst, si, ri, to)
        if cond is None:
            copy.start()
        else:
            pl.when(cond)(copy.start)

    def arrived(dst, ri, cond=None):
        copy = rc_(dst, dst, 0, ri, mate)
        if cond is None:
            copy.wait_recv()
        else:
            pl.when(cond)(copy.wait_recv)

    def local(src, dst, li=None):
        copy = pltpu.make_async_copy(src, dst, ls.at[lnum.take() if li is None else li])
        copy.start()
        return copy

    def landed(dst, li):
        pltpu.make_async_copy(dst, dst, ls.at[li]).wait()

    load_x = [lnum.take(), lnum.take()]
    for cc in range(2):
        local(x_hbm.at[:, :, cc, 0], xp.at[0, k, cc], load_x[0])
    load_we = local(we_hbm, we)
    load_b = local(b_hbm, b_ref)
    for cc in range(2):
        local(x_hbm.at[:, :, cc, 1], xp.at[1, k, cc], load_x[1])

    load_t = local(t_hbm, t_ref)

    barrier = pltpu.get_barrier_semaphore()
    peers = [dev(dz=1), dev(dz=-1), dev(flip=1)]
    peers += [dev(dy=d) for d in (1, 2, 3)] + [dev(dx=d) for d in (1, 2, 3)]
    across = [((z + 1) % 8, lat, 1 - k), ((z + 7) % 8, lat, 1 - k)]
    across_x = [(z, (x + d) % 4 * 4 + yh * 2 + c, 1 - k) for d in (1, 2, 3)]
    peers += across + across_x
    for to in peers:
        pl.semaphore_signal(barrier, inc=1, device_id=to, device_id_type=MESH)

    ku = [4, 4, 3 - k, 1 - k]
    kd = [3, 3 * (1 - k), 0, 0]
    route = []
    for m in range(4):
        s = 2 * m + k
        u, d = z - s, (s - z + 8) % 8
        on_up = jnp.logical_and(u >= 1, u <= ku[m])
        on_dn = jnp.logical_and(d >= 1, d <= kd[m])
        on = jnp.logical_or(on_up, on_dn)
        dist = jnp.where(on_up, u, d)
        reach = jnp.where(on_up, ku[m], kd[m])
        passing = jnp.logical_and(on_dn, z < s)
        next_passing = jnp.logical_and(on_dn, (z + 7) % 8 < s)
        next_passing = jnp.logical_and(next_passing, z > 0)
        route.append(dict(on=on, up=on_up, dn=on_dn, dist=dist, reach=reach, passing=passing,
                          next_passing=next_passing, valid=s <= z,
                          onward=jnp.where(on_up, 1, 7), back=jnp.where(on_up, 7, 1)))
    mine = z // 2
    home = k == h
    ku_own = jnp.where(mine == 0, 4, jnp.where(mine == 1, 4, jnp.where(mine == 2, 3 - h, 1 - h)))
    kd_own = jnp.where(mine == 0, 3, jnp.where(mine == 1, 3 * (1 - h), 0))
    home_up = jnp.logical_and(home, ku_own > 0)
    home_dn = jnp.logical_and(home, kd_own > 0)
    away = jnp.logical_not(home)
    away_up = jnp.logical_and(away, ku_own > 0)
    away_dn = jnp.logical_and(away, kd_own > 0)

    def clear():
        for m in range(4):
            @pl.when(jnp.logical_not(route[m]["valid"]))
            def _():
                latb[m] = jnp.zeros((512, 256), BF)

    lat_r = rnum.take(16 * SPLIT)
    mate_x, core_x, mate_t, mate_rec, mate_bias, line_x = (rnum.take() for _ in range(6))
    pg_r = rnum.take(4 * SPLIT)
    gr_r = rnum.take(20 * SPLIT)

    def lat_sem(m, q, j):
        return lat_r + m * (4 * SPLIT) + q * (2 * SPLIT) + j

    def rows(q, j):
        kk = k if j == 0 else 1 - k
        return pl.ds(pl.multiple_of(q * 256 + kk * 128, 128), 128)

    def some(q, j):
        kk = k if j < SPLIT else 1 - k
        return pl.ds(pl.multiple_of(q * 256 + kk * 128 + (j % SPLIT) * SUB, SUB), SUB)

    up_si, dn_si = group(own, home_up), group(own, home_dn)
    away_si, pg_si = group(own, away), group(pg, home)
    away_up_si, away_dn_si = group(own, away_up), group(own, away_dn)
    lat_si = [[snum.take() for m in range(3)] for q in range(2)]
    gr_si = [[snum.take() for m in range(4)] for q in range(2)]

    def origin_send(q, j):
        r = some(q, j)
        src = latb.at[mine, r]
        send(src, src, up_si, lat_sem(mine, q, j), dev(dz=1), home_up)
        slot = jnp.where(z >= 1, 4, mine)
        send(src, latb.at[slot, r], dn_si, lat_sem(mine, q, j), dev(dz=-1), home_dn)

    def gate(v):
        inner = 0.7978845608028654 * (v + 0.044715 * (v * v * v))
        t = jnp.tanh(inner)
        cdf = 0.5 * (1.0 + t)
        slope = cdf + 0.5 * v * (1.0 - t * t) * (0.7978845608028654 * (1.0 + 0.134145 * (v * v)))
        return v * cdf, slope

    def preact(q, kk):
        v = jnp.dot(xp[q, kk].reshape(128, 2048), we[...], preferred_element_type=F32) + b_ref[...]
        return gate(v)

    def encode(q):
        landed(xp.at[q, k], load_x[q])
        val, slope = preact(q, k)
        val = val.astype(BF)
        own[q] = val
        gp[rows(q, 0), :] = slope

        @pl.when(home)
        def _():
            latb[mine, rows(q, 0), :] = val

    def first_send(q):
        for j in range(SPLIT):
            src = own.at[q, j * SUB : j * SUB + SUB]
            dst, sem = latb.at[mine, some(q, j)], lat_sem(mine, q, SPLIT + j)
            dn_dst = latb.at[jnp.where(z >= 1, 4, mine), some(q, j)]
            send(src, dst, away_up_si, sem, across[0], away_up)
            send(src, dn_dst, away_dn_si, sem, across[1], away_dn)
            send(src, dst, away_si, sem, mate, away)
            origin_send(q, j)

    def send_inputs():
        load_t.wait()
        tg[pl.ds(k * 4 + x, 1)] = t_ref[:, pl.ds(mul(k, 1024), 512)][None]
        for hh in range(2):
            at = 8 + (k * 2 + yh) * 2 + hh
            tg[pl.ds(at, 1)] = t_ref[:, hh * 1024 + 512 : hh * 1024 + 1024][None]
        si = group(tg.at[0:13])
        slot = tg.at[k * 4 + x]
        here, there = pl.ds(mul(k, 1024), 512), pl.ds(mul(1 - k, 1024), 512)
        for d in (1, 2, 3):
            send(t_ref.at[:, here], slot, si, mate_t, dev(dx=d))
            send(t_ref.at[:, there], slot, si, mate_t, across_x[d - 1])
            for hh in range(2):
                at = 8 + (k * 2 + yh) * 2 + hh
                send(t_ref.at[:, hh * 1024 + 512 : hh * 1024 + 1024], tg.at[at], si, mate_t, dev(dy=d))
        send(t_ref.at[:, there], slot, si, mate_t, mate)
        part = xp.at[c, k, x // 2, x % 2]
        send(part, part, group(part), mate_x, mate)

    def spread_inputs():
        part = xp.at[c, 1 - k, x // 2, x % 2]
        arrived(part, mate_x)
        si = group(rx.at[0])
        for d in (1, 2, 3):
            send(part, part, si, line_x, dev(dx=d))

    def lat_hop(q, far):
        conds = []
        for m in range(3):
            e = route[m]
            cond = jnp.logical_and(e["on"], jnp.logical_and(e["dist"] == far, e["dist"] < e["reach"]))
            conds.append(cond)
            if not (far == 3 and m == 2):
                sent.append((lat_si[q][m], latb.at[0, 0:256], cond))
        for kk in range(2):
            for m in range(3):
                if far == 3 and m == 2:
                    continue
                e = route[m]

                @pl.when(conds[m])
                def _():
                    for j in range(kk * SPLIT, kk * SPLIT + SPLIT):
                        src = latb.at[jnp.where(e["passing"], 4, m), some(q, j)]
                        dst = latb.at[jnp.where(e["next_passing"], 4, m), some(q, j)]
                        arrived(src, lat_sem(m, q, j))
                        send(src, dst, lat_si[q][m], lat_sem(m, q, j), dev(dz=e["onward"]))

    def lat_last(q):
        for m in range(4):
            e = route[m]

            @pl.when(jnp.logical_and(e["on"], e["dist"] == e["reach"]))
            def _():
                for j in range(2 * SPLIT):
                    arrived(latb.at[m, some(q, j)], lat_sem(m, q, j))

        @pl.when(home)
        def _():
            for j in range(SPLIT, 2 * SPLIT):
                arrived(latb.at[mine, some(q, j)], lat_sem(mine, q, j))

    piece = {}
    for q in range(2):
        for ab in range(2):
            piece[q, ab] = {"core": rnum.take(), "a": rnum.take(), "b": rnum.take(), "g2": rnum.take(3), "g3": rnum.take()}

    def decode(q, ab):
        left = jnp.concatenate([latb[m, q * 256 : q * 256 + 256, :] for m in range(4)], axis=1)
        part = jnp.dot(left, wp[:, ab * 1024 : ab * 1024 + 1024], preferred_element_type=F32)
        p32[q, ab] = part.reshape(2, 2, 64, 1024)
        cs[q, ab] = p32[q, ab, :, o].astype(BF)
        send(cs.at[q, ab], cr.at[q, ab], group(cs.at[q, ab]), piece[q, ab]["core"], dev(flip=1))

    def stage_a(q):
        for ab in range(2):
            arrived(cr.at[q, ab], piece[q, ab]["core"])
            total = (p32[q, ab, :, c] + cr[q, ab].astype(F32)).reshape(4, 2, 16, 1024)
            s32[q, ab] = total
            ys[q, ab] = total.astype(BF)
            wide = ra.at[q] if ab == 0 else rb.at[q]
            si, sem = group(wide), piece[q, ab]["a"]
            for d in (1, 2, 3):
                if ab == 0:
                    to = (y + d) % 4
                    src = ys.at[q, 0, :, to // 2, :, pl.ds(mul(to % 2, 512), 512)]
                    send(src, ra.at[q, d - 1], si, sem, dev(dy=d))
                else:
                    send(ys.at[q, 1, (x + d) % 4], rb.at[q, d - 1], si, sem, dev(dx=d))

    def stage_b(q):
        for ab in range(2):
            buf = ra if ab == 0 else rb
            arrived(buf.at[q], piece[q, ab]["a"])
            if ab == 0:
                total = s32[q, 0, :, yh, :, pl.ds(mul(k, 512), 512)]
            else:
                total = s32[q, 1, x]
            for d in range(3):
                total = total + buf[q, d].astype(F32)
            if ab == 0:
                u32[q, 0] = total
                xs[q, 0] = total.astype(BF)
            else:
                for yy in range(4):
                    block = total[yy // 2, :, (yy % 2) * 512 : (yy % 2) * 512 + 512]
                    u32[q, 1, yy] = block
                    xs[q, 1, yy] = block.astype(BF)
            si, sem = group(rx.at[q, ab]), piece[q, ab]["b"]
            for d in (1, 2, 3):
                to = dev(dx=d) if ab == 0 else dev(dy=d)
                send(xs.at[q, ab], rx.at[q, ab, d - 1], si, sem, to)

    def line_of(q, ab, xx, yy):
        if ab == 0:
            cols = pl.ds(mul(yy % 2, 512), 512)
            return err.at[q, :, c, :, yy // 2, :, cols]
        return err.at[q, xx // 2, c, xx % 2, :, :, 1024:2048]

    def stage_c(q):
        for ab in range(2):
            arrived(rx.at[q, ab], piece[q, ab]["b"])
            total = u32[q, ab]
            for d in range(3):
                total = total + rx[q, ab, d].astype(F32)
            u32[q, ab] = total
            if ab == 0:
                diff = (total - tg[q * 4 : q * 4 + 4].astype(F32)).astype(BF)
                cols = pl.ds(mul(k, 512), 512)
                for xx in range(4):
                    err[q, xx // 2, c, xx % 2, yh, :, cols] = diff[xx]
            else:
                diff = (total - tg[8 + q * 4 : 12 + q * 4].astype(F32)).astype(BF)
                for yy in range(4):
                    start = 1024 + (yy % 2) * 512
                    err[q, x // 2, c, x % 2, yy // 2, :, start : start + 512] = diff[yy]
            line = line_of(q, ab, x, y)
            si = group(ra.at[q])
            for d in (1, 2, 3):
                to = dev(dy=d) if ab == 0 else dev(dx=d)
                send(line, line, si, piece[q, ab]["g2"] + d - 1, to)
            half = err.at[q, :, c, :, :, :, ab * 1024 : ab * 1024 + 1024]
            core_si[q, ab] = group(half)
            send(line, line, core_si[q, ab], piece[q, ab]["g3"], dev(flip=1))
            rc[q, :, ab * 512 : ab * 512 + 512] = u32[q, ab, x if ab == 0 else y].astype(BF)

    core_si = {}

    def stage_e(q):
        for d in (1, 3, 2):
            for ab in range(2):
                line = line_of(q, ab, (x - d + 4) % 4, (y - d + 4) % 4)
                arrived(line, piece[q, ab]["g2"] + d - 1)
                send(line, line, core_si[q, ab], piece[q, ab]["g3"], dev(flip=1))

    def stage_f(q):
        for ab in range(2):
            arrived(err.at[q, :, o, :, :, :, ab * 1024 : ab * 1024 + 1024], piece[q, ab]["g3"])

        for half in range(2):
            out = lax.dot_general(
                err[q].reshape(256, 2048), wp[half * 512 : half * 512 + 512, :],
                (((1,), (1,)), ((), ())), preferred_element_type=F32,
            )
            term[q, 2 * half] = out[:, :256]
            term[q, 2 * half + 1] = out[:, 256:]
            grad_step(q, 0, (2 * half, 2 * half + 1))

    def grad_step(q, depth, members=range(4)):
        for m in members:
            if depth > (3, 3, 2, 0)[m]:
                continue
            e = route[m]
            cond = jnp.logical_and(e["on"], e["reach"] - e["dist"] == depth)
            sent.append((gr_si[q][m], latb.at[0, 0:256], cond))

            @pl.when(cond)
            def _():
                slot = jnp.where(jnp.logical_and(e["dn"], e["dist"] == 1), 4, m)
                for j in range(2 * SPLIT):
                    sem = gr_r + m * (4 * SPLIT) + q * (2 * SPLIT) + j
                    r = slice(q * 256 + j * SUB, q * 256 + j * SUB + SUB)
                    part = term[q, m, j * SUB : j * SUB + SUB, :]
                    if depth:
                        arrived(gr.at[m, r], sem)
                        part = jnp.where(e["passing"], 0.0, part) + gr[m, r, :].astype(F32)
                    gs[m, r, :] = part.astype(BF)
                    sem = gr_r + slot * (4 * SPLIT) + q * (2 * SPLIT) + j
                    send(gs.at[m, r], gr.at[slot, r], gr_si[q][m], sem, dev(dz=e["back"]))

    def finish(q):
        for j in range(2 * SPLIT):
            i = q * 2 * SPLIT + j
            r = slice(i * SUB, i * SUB + SUB)

            @pl.when(home)
            def _():
                lg[...] = term[q, mine, j * SUB : j * SUB + SUB, :]

            @pl.when(home_up)
            def _():
                arrived(gr.at[mine, r], gr_r + mine * (4 * SPLIT) + i)
                lg[...] += gr[mine, r, :].astype(F32)

            @pl.when(home_dn)
            def _():
                arrived(gr.at[4, r], gr_r + 16 * SPLIT + i)
                lg[...] += gr[4, r, :].astype(F32)

            @pl.when(home)
            def _():
                grad = lg[...] * gp[r, :]
                pg[r, :] = grad.astype(BF)
                total = jnp.sum(grad, axis=0, keepdims=True)
                if i == 0:
                    bs[...] = jnp.broadcast_to(total, (8, 256))
                else:
                    bs[...] += jnp.broadcast_to(total, (8, 256))
                send(pg.at[r], pg.at[r], pg_si, pg_r + i, mate)

    def flip_inputs(q, j):
        kk = k if j == 0 else 1 - k
        for i in range(2):
            block = xp[q, kk, :, :, :, :, i * 1024 : i * 1024 + 1024].reshape(128, 1024)
            xt[i * 1024 : i * 1024 + 1024, rows(q, j)] = block.T

    def flip_latents(q):
        for m in range(4):
            lt[m * 256 : m * 256 + 256, q * 256 : q * 256 + 256] = latb[m, q * 256 : q * 256 + 256, :].T

    def decoder_grads():
        def part(i, _):
            right = err[:, :, :, :, :, :, pl.ds(mul(i, 512), 512)].reshape(512, 512)
            start = pl.multiple_of((i % 2) * 1024 + (i // 2) * 512, 512)
            dec_out[:, pl.ds(start, 512)] = jnp.dot(lt[...], right, preferred_element_type=F32).astype(BF)
            return 0

        lax.fori_loop(0, 4, part, 0)

    load_we.wait()
    load_b.wait()
    encode(0)
    pl.semaphore_wait(barrier, len(peers))
    first_send(0)
    encode(1)
    first_send(1)
    load_w = lnum.take()
    for ab in range(2):
        for hh in range(2):
            local(
                w_hbm.at[:, hh * 1024 + ab * 512 : hh * 1024 + ab * 512 + 512],
                wp.at[:, ab * 1024 + hh * 512 : ab * 1024 + hh * 512 + 512],
                load_w,
            )
    send_inputs()
    clear()
    lat_hop(0, 1)
    lat_hop(1, 1)
    flip_inputs(0, 0)
    lat_hop(0, 2)
    lat_hop(1, 2)
    spread_inputs()
    flip_inputs(1, 0)
    lat_hop(0, 3)
    lat_hop(1, 3)
    lat_last(0)
    landed(wp, load_w)
    decode(0, 0)
    decode(0, 1)
    lat_last(1)
    decode(1, 0)
    stage_a(0)
    decode(1, 1)
    flip_latents(0)
    stage_a(1)
    flip_latents(1)
    arrived(rx.at[0], line_x)
    send(xp.at[c, 1 - k], xp.at[c, 1 - k], group(xp.at[c, 1 - k]), core_x, dev(flip=1))
    stage_b(0)
    stage_b(1)
    arrived(tg.at[0:13], mate_t)
    arrived(xp.at[o, 1 - k], core_x)
    for q in range(2):
        gp[rows(q, 1), :] = preact(q, 1 - k)[1]
    stage_c(0)
    stage_c(1)
    flip_inputs(0, 1)
    flip_inputs(1, 1)
    stage_e(0)
    stage_e(1)
    stage_f(0)
    stage_f(1)
    recs[:, pl.ds(mul(k, 1024), 1024)] = rc[k]
    send(rc.at[1 - k], recs.at[:, pl.ds(mul(k, 1024), 1024)], group(rc.at[1 - k]), mate_rec, mate)
    pl.when(z < 4)(decoder_grads)
    grad_step(0, 1)
    grad_step(1, 1)
    grad_step(0, 2)
    grad_step(1, 2)
    grad_step(0, 3)
    grad_step(1, 3)
    pl.when(z >= 4)(decoder_grads)
    finish(0)
    finish(1)
    send(bs, bs, group(bs, home), mate_bias, mate, home)
    for i in range(4 * SPLIT):
        arrived(pg.at[i * SUB : i * SUB + SUB], pg_r + i, away)

    pg_out[...] = pg[...]
    arrived(bs, mate_bias, away)
    bias_out[...] = bs[0:1, :]
    arrived(recs.at[:, pl.ds(mul(1 - k, 1024), 1024)], mate_rec)
    rec_out[...] = recs[...]
    for si, like, cond in sent:
        copy = rc_(like, like, si, 0, mate)
        if cond is None:
            copy.wait_send()
        else:
            pl.when(cond)(copy.wait_send)
    assert (snum.count, rnum.count, lnum.count) == COUNTS, (snum.count, rnum.count, lnum.count)


def outputs(rec_in, bias_in, pg, xt, dec_in, rec, enc, bias, dec, encv, sem):
    copies = [
        pltpu.make_async_copy(dec_in, dec, sem.at[0]),
        pltpu.make_async_copy(rec_in, rec, sem.at[1]),
        pltpu.make_async_copy(bias_in, bias, sem.at[2]),
        pltpu.make_async_copy(encv, enc, sem.at[3]),
    ]
    for copy in copies[:3]:
        copy.start()
    encv[...] = jnp.dot(xt[...], pg[...], preferred_element_type=F32).astype(BF)
    copies[3].start()
    for copy in copies:
        copy.wait()


def kernel1(layer_inputs, layer_targets, encoder_weight, encoder_bias, decoder_weight):
    vm, hbm = pl.BlockSpec(memory_space=pltpu.VMEM), pl.BlockSpec(memory_space=pl.ANY)
    scratch = [
        pltpu.VMEM((16, 2048), BF),
        pltpu.VMEM((1, 256), F32),
        pltpu.VMEM((2, 2, 2, 2, 2, 16, 2048), BF),
        pltpu.VMEM((2048, 256), BF),
        pltpu.VMEM((1024, 2048), BF),
        pltpu.VMEM((2, 128, 256), BF),
        pltpu.VMEM((5, 512, 256), BF),
        pltpu.VMEM((1024, 512), BF),
        pltpu.VMEM((512, 256), F32),
        pltpu.VMEM((16, 16, 512), BF),
        pltpu.VMEM((2, 2, 2, 2, 64, 1024), F32),
        pltpu.VMEM((2, 2, 2, 64, 1024), BF),
        pltpu.VMEM((2, 2, 2, 64, 1024), BF),
        pltpu.VMEM((2, 2, 4, 2, 16, 1024), F32),
        pltpu.VMEM((2, 2, 4, 2, 16, 1024), BF),
        pltpu.VMEM((2, 3, 4, 16, 512), BF),
        pltpu.VMEM((2, 3, 2, 16, 1024), BF),
        pltpu.VMEM((2, 2, 4, 16, 512), F32),
        pltpu.VMEM((2, 2, 4, 16, 512), BF),
        pltpu.VMEM((2, 2, 3, 4, 16, 512), BF),
        pltpu.VMEM((2, 16, 1024), BF),
        pltpu.VMEM((2, 2, 2, 2, 2, 16, 2048), BF),
        pltpu.VMEM((2, 4, 256, 256), F32),
        pltpu.VMEM((5, 512, 256), BF),
        pltpu.VMEM((4, 512, 256), BF),
        pltpu.VMEM((SUB, 256), F32),
        pltpu.VMEM((512, 256), BF),
        pltpu.VMEM((8, 256), F32),
        pltpu.VMEM((16, 2048), BF),
        *[pltpu.SemaphoreType.DMA((n,)) for n in COUNTS],
    ]
    rec, bias, pg, xt, dec = pl.pallas_call(
        kernel,
        out_shape=(
            pltpu.VMEM((16, 2048), BF),
            pltpu.VMEM((1, 256), F32),
            pltpu.VMEM((512, 256), BF),
            pltpu.VMEM((2048, 512), BF),
            pltpu.VMEM((1024, 2048), BF),
        ),
        in_specs=[hbm] * 5,
        out_specs=[vm] * 5,
        scratch_shapes=scratch,
        compiler_params=pltpu.CompilerParams(
            collective_id=0, has_side_effects=True, vmem_limit_bytes=48 * 1024 * 1024
        ),
        name="transcoder_step",
    )(
        layer_inputs.reshape(2, 2, 2, 2, 16, 2048),
        layer_targets[0],
        encoder_weight[0],
        encoder_bias,
        decoder_weight.reshape(1024, 2048),
    )
    return rec, bias, pg, xt, dec


def shards(*args):
    vm, hbm = pl.BlockSpec(memory_space=pltpu.VMEM), pl.BlockSpec(memory_space=pl.ANY)
    rec, bias, pg, xt, dec = kernel1(*args)
    rec, enc, bias, dec = pl.pallas_call(
        outputs,
        out_shape=(
            jax.ShapeDtypeStruct((16, 2048), BF),
            jax.ShapeDtypeStruct((2048, 256), BF),
            jax.ShapeDtypeStruct((1, 256), F32),
            jax.ShapeDtypeStruct((1024, 2048), BF),
        ),
        in_specs=[vm] * 5,
        out_specs=[hbm] * 4,
        scratch_shapes=[pltpu.VMEM((2048, 256), BF), pltpu.SemaphoreType.DMA((4,))],
        compiler_params=pltpu.CompilerParams(vmem_limit_bytes=16 * 1024 * 1024),
        name="write_outputs",
    )(rec, bias, pg, xt, dec)
    return rec[None], enc[None], bias, dec.reshape(1, 4, 1, 256, 2048)


def solution(mesh):
    placed = (
        P("layer", "tok", None),
        P("layer", ("latent", "tok"), None),
        P("layer", None, "latent"),
        P("layer", "latent"),
        P("layer", None, "tok", "latent", None),
    )
    return jax.shard_map(
        shards,
        mesh=mesh,
        in_specs=placed,
        out_specs=(
            P("layer", ("latent", "tok"), None),
            P("layer", None, "latent"),
            P("layer", "latent"),
            P("layer", None, "tok", "latent", None),
        ),
        check_vma=False,
    )
```
